128 devices in a mesh: row: 32 (over z, y, core), ctr: 4 (over x).
Axes of the slice: x: 4, y: 4, z: 4, core: 2. Of those that a mesh axis runs over, the one named last changes fastest.
Arguments:
- embeddings: bfloat16 [98304, 1536], P(('row', 'ctr')), may hold values from -7 to 7
- centroids: bfloat16 [512, 256, 1536], P('row', 'ctr'), may hold values from -6 to 6
- candidates: int32 [128, 6], P(('row', 'ctr')), may hold values from 0 to 511, as said below
Outputs:
- new_centroids: bfloat16 [512, 256, 1536], P('row', 'ctr')
- nearest: float32 [98304], P(('row', 'ctr'))
The draws below stay inside these ranges and needn't reach their ends.
Inputs may be any that keep to these rules, and one draw needn't show every extreme that they name: `candidates`: block b is owned by index b // 16 of row. Each row names 6 blocks of 6 different owners. The 4 row blocks of one index of row name at most one block of each owner (the same block wherever that owner appears).
All inputs are finite; a program needn't handle non-finite values.
Results may differ from the reference program's by a relative error of at most 0.007.
Values may be sent and summed in bfloat16 or wider, within the bound.
A program may use at most 128 MiB of HBM per device.

```python
import math
import jax
import jax.numpy as jnp
from jax import lax

EMBED_WIDTH = 1536
CENTROID_BLOCK = 256
RB = 768
CANDIDATE_BLOCKS = 6
BLK_GRP = 16
NRB = 128
NBLK = 512
ROWS = 98304
N_ROW = 32
N_CTR = 4


def draw_lists(key):
    key = jax.random.fold_in(key, 101)
    draw_one = jax.random.randint(jax.random.fold_in(key, 1), (N_ROW, N_ROW), 0, BLK_GRP)
    draw_two = jax.random.randint(jax.random.fold_in(key, 2), (N_ROW, N_ROW), 0, BLK_GRP)
    local_idx = BLK_GRP - 1 - draw_one * draw_two // (BLK_GRP - 1)
    weight = jax.random.randint(jax.random.fold_in(key, 3), (N_ROW,), 1, 5)
    jitter = jax.random.randint(jax.random.fold_in(key, 4), (NRB, N_ROW), 0, 65536)
    ranking = jitter * weight[None, :] * N_ROW + jnp.arange(N_ROW)[None, :]
    _, owners = lax.top_k(ranking, CANDIDATE_BLOCKS)
    group_of = jnp.arange(NRB) // N_CTR
    chosen = jnp.take_along_axis(local_idx[group_of], owners, axis=1)
    return (owners * BLK_GRP + chosen).astype(jnp.int32)


def raw_rows(key):
    key = jax.random.fold_in(key, 201)
    normal_part = jax.random.truncated_normal(jax.random.fold_in(key, 1), -6.0, 6.0, (ROWS, EMBED_WIDTH))
    return normal_part


def draw_candidates(key, part):
    return draw_lists(key)


def draw_embeddings(key, part):
    values = raw_rows(key)
    return values.astype(jnp.bfloat16)


def draw_centroids(key, part):
    own_key = jax.random.fold_in(key, 301)
    initial = jax.random.truncated_normal(own_key, -4.0, 4.0, (NBLK, CENTROID_BLOCK, EMBED_WIDTH)) / math.sqrt(EMBED_WIDTH)
    return initial.astype(jnp.bfloat16)


def setup_inputs(seed: int = 0) -> dict:
    arg_keys = jax.random.split(jax.random.key(seed), 4)
    embeddings = draw_embeddings(jax.random.fold_in(arg_keys[3], 71), 0)
    centroids = draw_centroids(jax.random.fold_in(arg_keys[3], 71), 0)
    candidates = draw_candidates(jax.random.fold_in(arg_keys[3], 71), 0)
    return {"embeddings": embeddings, "centroids": centroids, "candidates": candidates}


score_scale = 1.5
epsilon = 1e-06

def normalize(embeddings):
    values = embeddings.astype(jnp.float32)
    return (values * lax.rsqrt(lax.optimization_barrier(jnp.mean(values * values, axis=-1, keepdims=True)) + epsilon)).astype(jnp.bfloat16)

def reference(embeddings, centroids, candidates):
    normed = normalize(embeddings)
    group_rows = normed.reshape(N_ROW, N_CTR, RB, EMBED_WIDTH)
    group_lists = candidates.reshape(N_ROW, N_CTR, CANDIDATE_BLOCKS)
    order_ids = jnp.arange(N_CTR * CANDIDATE_BLOCKS)
    earlier = order_ids[:, None] > order_ids[None, :]

    def one_group(running, element):
        row_data, list_ids = element
        picked = centroids[list_ids].astype(jnp.float32)
        scores = score_scale * jnp.einsum('qrd,qjkd->qrjk', row_data.astype(jnp.float32), picked)
        highest = lax.optimization_barrier(jnp.max(scores, axis=(2, 3), keepdims=True))
        exponent = jnp.exp(scores - highest)
        weights = (exponent / lax.optimization_barrier(jnp.sum(exponent, axis=(2, 3), keepdims=True))).astype(jnp.bfloat16)
        contribution = jnp.einsum('qrjk,qrd->qjkd', weights.astype(jnp.float32), row_data.astype(jnp.float32))
        flat_ids = list_ids.reshape(-1)
        identical_index = (flat_ids[:, None] == flat_ids[None, :]).astype(jnp.float32)
        merged_result = jnp.einsum('ex,xmg->emg', identical_index, contribution.reshape(N_CTR * CANDIDATE_BLOCKS, CENTROID_BLOCK, EMBED_WIDTH), precision=lax.Precision.HIGHEST).astype(jnp.bfloat16)
        leading = jnp.logical_not(jnp.any(jnp.logical_and(identical_index > 0, earlier), axis=1))
        retained = jnp.where(leading[:, None, None], merged_result.astype(jnp.float32), jnp.zeros((), jnp.float32))
        return (running.at[flat_ids].add(retained), None)
    start = jnp.zeros((NBLK, CENTROID_BLOCK, EMBED_WIDTH), jnp.float32)
    sums, _ = lax.scan(one_group, start, (group_rows, group_lists))
    new_centroids = (sums * lax.rsqrt(lax.optimization_barrier(jnp.mean(sums * sums, axis=-1, keepdims=True)) + epsilon) / math.sqrt(EMBED_WIDTH)).astype(jnp.bfloat16)

    def rescore(running, element):
        row_data, list_ids = element
        picked = new_centroids[list_ids].astype(jnp.float32)
        similar = jnp.einsum('qrd,qjkd->qrjk', row_data.astype(jnp.float32), picked)
        return (running, lax.optimization_barrier(jnp.max(similar, axis=(2, 3))))
    _, nearest = lax.scan(rescore, jnp.zeros((), jnp.float32), (group_rows, group_lists))
    return (new_centroids, nearest.reshape(ROWS))
```

```python
import functools
import math

import jax
import jax.numpy as jnp
from jax import lax
from jax.experimental import pallas as pl
from jax.experimental.pallas import tpu as pltpu
from jax.sharding import PartitionSpec as P

score_scale = 1.5
epsilon = 1e-06
MESH = pl.DeviceIdType.MESH

N_Z, N_Y, N_C = 4, 4, 2
N_ROW = N_Z * N_Y * N_C
N_CTR = 4
CANDS = 6
PIECES = 4


def shifted(row, k, sign):
    z, y, c = row // 8, (row // 2) % 4, row % 2
    dz, dy, dc = k // 8, (k // 2) % 4, k % 2
    return (
        lax.rem(z + sign * dz + 4, 4) * 8
        + lax.rem(y + sign * dy + 4, 4) * 2
        + lax.rem(c + sign * dc + 2, 2)
    )


def kernel(
    wanted, slot_of, j_of, sorted_k, same, last,
    emb_in, cent_in,
    new_out, near_out,
    rows, cent, stage, back, b0, b1, b2, b3, c0, c1, c2, c3,
    ex, wts, stat, wb, cum, f0, f1, f2, f3, st, bb, rb,
    loc_sem, xs, xr, s1, r1, s2, r2, s3, r3, ss, sr, ns, nr, out_sem,
):
    row, ctr = lax.axis_index("row"), lax.axis_index("ctr")
    fetched = (b0, b1, b2, b3)
    landed = (c0, c1, c2, c3)
    fresh = (f0, f1, f2, f3)
    RB = rows.shape[0] // N_CTR
    D = rows.shape[1]
    H = cent.shape[1] // PIECES
    CB = cent.shape[1]
    Q = RB // 4

    emb_copy = pltpu.make_async_copy(emb_in, rows.at[pl.ds(0, RB)], loc_sem.at[0])
    cent_copy = pltpu.make_async_copy(cent_in, cent, loc_sem.at[1])
    emb_copy.start()
    cent_copy.start()

    barrier = pltpu.get_barrier_semaphore()

    def greet(k, carry):
        pl.semaphore_signal(
            barrier, inc=1, device_id=(shifted(row, k, 1), ctr), device_id_type=MESH
        )
        return carry

    lax.fori_loop(1, N_ROW, greet, 0)
    for d in range(1, N_CTR):
        pl.semaphore_signal(
            barrier, inc=1, device_id=(row, lax.rem(ctr + d, N_CTR)), device_id_type=MESH
        )
    pl.semaphore_wait(barrier, N_ROW - 1 + N_CTR - 1)

    right = (row, lax.rem(ctr + 1, N_CTR))
    left = (row, lax.rem(ctr + 3, N_CTR))

    def row_copy(src, dst, part, device, sem):
        return pltpu.make_async_remote_copy(
            src_ref=rows.at[pl.ds(src * RB + part * Q, Q)],
            dst_ref=rows.at[pl.ds(dst * RB + part * Q, Q)],
            send_sem=xs.at[sem],
            recv_sem=xr.at[sem],
            device_id=device,
            device_id_type=MESH,
        )

    to_right = [row_copy(0, 1, part, right, part) for part in range(4)]
    to_left = [row_copy(0, 3, part, left, 4 + part) for part in range(4)]
    onward = [
        row_copy(1, 2, 0, right, 8),
        row_copy(1, 2, 1, right, 9),
        row_copy(3, 2, 2, left, 10),
        row_copy(3, 2, 3, left, 11),
    ]

    emb_copy.wait()
    for one, two in zip((0, 1, 2, 3), (2, 3, 0, 1)):
        if one < 2:
            for part in (one, two):

                def normalise(t, carry):
                    place = pl.ds(pl.multiple_of(part * Q + t * 64, 64), 64)
                    values = rows[place, :].astype(jnp.float32)
                    scale = lax.rsqrt(jnp.mean(values * values, axis=-1, keepdims=True) + epsilon)
                    rows[place, :] = (values * scale).astype(jnp.bfloat16)
                    return carry

                lax.fori_loop(0, Q // 64, normalise, 0)
        to_right[one].start()
        to_left[two].start()

    def slot_send(src, dst, k, sign, send, recv):
        return pltpu.make_async_remote_copy(
            src_ref=src,
            dst_ref=dst,
            send_sem=send,
            recv_sem=recv,
            device_id=(shifted(row, k, sign), ctr),
            device_id_type=MESH,
        )

    def all_slots(buf_send, buf_recv, send, recv):
        others = pl.ds(1, N_ROW - 1)
        return pltpu.make_async_remote_copy(
            src_ref=buf_send.at[others],
            dst_ref=buf_recv.at[others],
            send_sem=send,
            recv_sem=recv,
            device_id=(row, ctr),
            device_id_type=MESH,
        )

    cent_copy.wait()
    for i in range(PIECES):

        def fetch(t, carry):
            k = lax.rem(t * 5, N_ROW)
            block = jnp.maximum(wanted[k], 0)
            stage[i, k] = cent[block, i * H : (i + 1) * H, :]

            @pl.when(k != 0)
            def _():
                slot_send(stage.at[i, k], fetched[i].at[k], k, 1, s1.at[i], r1.at[i]).start()

            return carry

        lax.fori_loop(0, N_ROW, fetch, 0)
        fetched[i][0] = stage[i, 0]

    to_right[0].wait_recv()
    onward[0].start()
    to_left[2].wait_recv()
    onward[2].start()
    to_right[1].wait_recv()
    onward[1].start()
    to_left[3].wait_recv()
    onward[3].start()
    for i in range(PIECES):
        done = all_slots(stage.at[i], fetched[i], s1.at[i], r1.at[i])
        done.wait_send()
        done.wait_recv()

    def scores_of(s):
        def pick(j, carry):
            slot = slot_of[s * CANDS + j]
            for i in range(PIECES):
                stat[pl.ds(pl.multiple_of(j * CB + i * H, H), H), :] = fetched[i][slot]
            return carry

        lax.fori_loop(0, CANDS, pick, 0)

        def tile(n, carry):
            place = pl.ds(pl.multiple_of(n * 256, 256), 256)
            near = pl.ds(pl.multiple_of(s * RB + n * 256, 256), 256)
            score = score_scale * lax.dot_general(
                stat[...], rows[near, :], (((1,), (1,)), ((), ())),
                preferred_element_type=jnp.float32,
            )
            top = jnp.max(score, axis=0, keepdims=True)
            power = jnp.exp(score - top)
            ex[s, :, place] = power
            st[0, s : s + 1, place] = top
            st[0, N_CTR + s : N_CTR + s + 1, place] = jnp.sum(power, axis=0, keepdims=True)
            return carry

        lax.fori_loop(0, RB // 256, tile, 0)

    scores_of(0)
    to_right[2].wait_recv()
    to_right[3].wait_recv()
    scores_of(1)
    to_left[0].wait_recv()
    to_left[1].wait_recv()
    scores_of(3)
    for copy in onward:
        copy.wait_recv()
    scores_of(2)
    for copy in to_right + to_left + onward:
        copy.wait_send()

    stat_sends = [
        pltpu.make_async_remote_copy(
            src_ref=st.at[0],
            dst_ref=st.at[d],
            send_sem=ss.at[d],
            recv_sem=sr.at[d],
            device_id=(row, lax.rem(ctr + d, N_CTR)),
            device_id_type=MESH,
        )
        for d in range(1, N_CTR)
    ]
    for copy in stat_sends:
        copy.start()
    for s in range(N_CTR):
        wts[s, CANDS] = jnp.zeros(wts.shape[2:], wts.dtype)
    for copy in stat_sends:
        copy.wait()
    for s in range(N_CTR):
        tops = [st[d, (s - d) % N_CTR : (s - d) % N_CTR + 1, :] for d in range(N_CTR)]
        totals = [
            st[d, N_CTR + (s - d) % N_CTR : N_CTR + (s - d) % N_CTR + 1, :] for d in range(N_CTR)
        ]
        highest = functools.reduce(jnp.maximum, tops)
        total = functools.reduce(
            jnp.add, [total * jnp.exp(top - highest) for top, total in zip(tops, totals)]
        )
        factor = jnp.exp(tops[0] - highest) / total

        def weigh(j, carry):
            place = pl.ds(pl.multiple_of(j * CB, CB), CB)
            wts[s, j] = (ex[s, place, :] * factor).astype(jnp.bfloat16)
            return carry

        lax.fori_loop(0, CANDS, weigh, 0)

    half = N_ROW // 2
    for i in range(PIECES):
        for h in range(2):

            def lay(t, carry):
                for s in range(N_CTR):
                    j = j_of[(h * half + t) * N_CTR + s]
                    wb[pl.ds(pl.multiple_of(t * H, H), H), s * RB : (s + 1) * RB] = wts[
                        s, j, i * H : (i + 1) * H, :
                    ]
                return carry

            lax.fori_loop(0, half, lay, 0)

            def multiply(n, carry):
                place = pl.ds(pl.multiple_of(n * 256, 256), 256)
                total = jnp.dot(wb[...], rows[:, place], preferred_element_type=jnp.float32)
                stage[i, h * half : (h + 1) * half, :, place] = total.reshape(half, H, 256).astype(
                    jnp.bfloat16
                )
                return carry

            lax.fori_loop(0, D // 256, multiply, 0)

            def deliver(t, carry):
                k = h * half + lax.rem(t * 5, half)

                @pl.when(k != 0)
                def _():
                    slot_send(stage.at[i, k], landed[i].at[k], k, -1, s2.at[i], r2.at[i]).start()

                return carry

            lax.fori_loop(0, half, deliver, 0)
        landed[i][0] = stage[i, 0]

    out_copies = []
    for i in range(PIECES):
        all_slots(stage.at[i], landed[i], s2.at[i], r2.at[i]).wait_recv()

        def add(t, total):
            keep = same[t].astype(jnp.float32)
            total = landed[i][sorted_k[t]].astype(jnp.float32) + total * keep
            cum[t] = total
            return total

        lax.fori_loop(0, N_ROW, add, jnp.zeros((H, D), jnp.float32))

        def renew(b, carry):
            end = last[b]
            total = cum[jnp.maximum(end, 0)]
            total = jnp.where(end >= 0, total, jnp.zeros_like(total))
            scale = lax.rsqrt(jnp.mean(total * total, axis=-1, keepdims=True) + epsilon)
            fresh[i][b] = (total * scale * (1.0 / math.sqrt(D))).astype(jnp.bfloat16)
            return carry

        lax.fori_loop(0, cent.shape[0], renew, 0)

        def give(t, carry):
            k = lax.rem(t * 5, N_ROW)
            back[i, k] = fresh[i][jnp.maximum(wanted[k], 0)]

            @pl.when(k != 0)
            def _():
                slot_send(back.at[i, k], fetched[i].at[k], k, 1, s3.at[i], r3.at[i]).start()

            return carry

        lax.fori_loop(0, N_ROW, give, 0)
        fetched[i][0] = back[i, 0]
        out = pltpu.make_async_copy(
            fresh[i], new_out.at[:, pl.ds(i * H, H)], out_sem.at[i]
        )
        out.start()
        out_copies.append(out)

    for i in range(PIECES):
        all_slots(back.at[i], fetched[i], s3.at[i], r3.at[i]).wait_recv()
        for s in range(N_CTR):
            for j in range(CANDS):
                stat[j * H : (j + 1) * H, :] = fetched[i][slot_of[s * CANDS + j]]

            def tile(n, carry):
                place = pl.ds(pl.multiple_of(n * 256, 256), 256)
                near = pl.ds(pl.multiple_of(s * RB + n * 256, 256), 256)
                similar = lax.dot_general(
                    stat[0 : CANDS * H, :], rows[near, :], (((1,), (1,)), ((), ())),
                    preferred_element_type=jnp.float32,
                )
                best = jnp.max(similar, axis=0, keepdims=True)
                if i > 0:
                    best = jnp.maximum(best, bb[s, 0:1, place])
                bb[s, :, place] = jnp.broadcast_to(best, (8, 256))
                return carry

            lax.fori_loop(0, RB // 256, tile, 0)
    best_sends = [
        pltpu.make_async_remote_copy(
            src_ref=bb.at[d],
            dst_ref=rb.at[d],
            send_sem=ns.at[d],
            recv_sem=nr.at[d],
            device_id=(row, lax.rem(ctr - d + N_CTR, N_CTR)),
            device_id_type=MESH,
        )
        for d in range(1, N_CTR)
    ]
    for copy in best_sends:
        copy.start()
    for i in range(PIECES):
        all_slots(stage.at[i], landed[i], s2.at[i], r2.at[i]).wait_send()
        all_slots(back.at[i], fetched[i], s3.at[i], r3.at[i]).wait_send()
        out_copies[i].wait()
    for copy in best_sends:
        copy.wait()
    best = bb[0, 0:1, :]
    for d in range(1, N_CTR):
        best = jnp.maximum(best, rb[d, 0:1, :])
    near_out[...] = best


def tables(candidates, blocks_held):
    row, ctr = lax.axis_index("row"), lax.axis_index("ctr")
    lists = lax.all_gather(candidates, ("row", "ctr"), axis=0, tiled=True).reshape(
        N_ROW, N_CTR, CANDS
    )
    ks = jnp.arange(N_ROW, dtype=jnp.int32)
    ahead, behind = shifted(row, ks, 1), shifted(row, ks, -1)
    asking = jnp.where(lists // blocks_held == row, lists % blocks_held, -1).max(axis=(1, 2))
    wanted = jnp.sum(jnp.where(ahead[:, None] == ks, asking[None, :] + 1, 0), axis=1) - 1
    mine = lax.dynamic_index_in_dim(lists, row, 0, keepdims=False) // blocks_held
    turn = (ctr - jnp.arange(N_CTR)) % N_CTR
    mine = jnp.sum(jnp.where(turn[:, None, None] == jnp.arange(N_CTR)[:, None], mine[None], 0), axis=1)
    hit = mine[:, :, None] == behind
    slot_of = jnp.sum(jnp.where(hit, ks, 0), axis=2).reshape(-1)
    js = jnp.arange(CANDS, dtype=jnp.int32)[None, :, None]
    j_of = CANDS + jnp.sum(jnp.where(hit, js - CANDS, 0), axis=1).T.reshape(-1)
    key = jnp.where(wanted < 0, blocks_held, wanted) * N_ROW + ks
    rank = jnp.sum((key[None, :] < key[:, None]).astype(jnp.int32), axis=1)
    at = rank[None, :] == ks[:, None]
    sorted_k = jnp.sum(jnp.where(at, ks, 0), axis=1)
    sorted_w = jnp.sum(jnp.where(at, wanted, 0), axis=1)
    before = jnp.sum(jnp.where(rank[None, :] == ks[:, None] - 1, wanted, 0), axis=1)
    same = jnp.logical_and(sorted_w == before, ks > 0).astype(jnp.int32)
    blocks = jnp.arange(blocks_held, dtype=jnp.int32)
    named = wanted[None, :] == blocks[:, None]
    last = jnp.max(jnp.where(named, rank[None, :], -1), axis=1)
    return [t.astype(jnp.int32) for t in (wanted, slot_of, j_of, sorted_k, same, last)]


def on_device(embeddings, centroids, candidates):
    blocks, width, features = centroids.shape
    rb = embeddings.shape[0]
    held = width // PIECES
    info = tables(candidates, blocks)
    bf16, f32 = jnp.bfloat16, jnp.float32
    piece = pltpu.VMEM((N_ROW, held, features), bf16)
    dma = pltpu.SemaphoreType.DMA
    renewed, nearest = pl.pallas_call(
        kernel,
        out_shape=(
            jax.ShapeDtypeStruct(centroids.shape, bf16),
            jax.ShapeDtypeStruct((1, rb), f32),
        ),
        in_specs=[pl.BlockSpec(memory_space=pltpu.SMEM)] * 6
        + [pl.BlockSpec(memory_space=pl.ANY)] * 2,
        out_specs=(
            pl.BlockSpec(memory_space=pl.ANY),
            pl.BlockSpec(memory_space=pltpu.VMEM),
        ),
        scratch_shapes=[
            pltpu.VMEM((N_CTR * rb, features), bf16),
            pltpu.VMEM((blocks, width, features), bf16),
            pltpu.VMEM((PIECES, N_ROW, held, features), bf16),
            pltpu.VMEM((PIECES, N_ROW, held, features), bf16),
            *([piece] * 8),
            pltpu.VMEM((N_CTR, CANDS * width, rb), f32),
            pltpu.VMEM((N_CTR, CANDS + 1, width, rb), bf16),
            pltpu.VMEM((CANDS * width, features), bf16),
            pltpu.VMEM((N_ROW // 2 * held, N_CTR * rb), bf16),
            pltpu.VMEM((N_ROW, held, features), f32),
            *([pltpu.VMEM((blocks, held, features), bf16)] * 4),
            pltpu.VMEM((N_CTR, 2 * N_CTR, rb), f32),
            pltpu.VMEM((N_CTR, 8, rb), f32),
            pltpu.VMEM((N_CTR, 8, rb), f32),
            dma((2,)),
            dma((12,)),
            dma((12,)),
            *([dma((PIECES,))] * 6),
            *([dma((N_CTR,))] * 4),
            dma((PIECES,)),
        ],
        compiler_params=pltpu.CompilerParams(
            collective_id=0, has_side_effects=True, vmem_limit_bytes=60 * 2**20
        ),
    )(*info, embeddings, centroids)
    return renewed, nearest.reshape(rb)


def solution(mesh):
    in_specs = (P(("row", "ctr"), None), P("row", "ctr", None), P(("row", "ctr"), None))
    out_specs = (P("row", "ctr", None), P(("row", "ctr")))
    return jax.shard_map(
        on_device, mesh=mesh, in_specs=in_specs, out_specs=out_specs, check_vma=False
    )
```

```python
import functools
import math

import jax
import jax.numpy as jnp
from jax import lax
from jax.experimental import pallas as pl
from jax.experimental.pallas import tpu as pltpu
from jax.sharding import PartitionSpec as P

score_scale = 1.5
epsilon = 1e-06
MESH = pl.DeviceIdType.MESH

N_Z, N_Y, N_C = 4, 4, 2
N_ROW = N_Z * N_Y * N_C
N_CTR = 4
CANDS = 6
PIECES = 4


def shifted(row, k, sign):
    z, y, c = row // 8, (row // 2) % 4, row % 2
    dz, dy, dc = k // 8, (k // 2) % 4, k % 2
    return (
        lax.rem(z + sign * dz + 4, 4) * 8
        + lax.rem(y + sign * dy + 4, 4) * 2
        + lax.rem(c + sign * dc + 2, 2)
    )


def steps_from(owner, row):
    dz = (row // 8 - owner // 8 + 4) % 4
    dy = ((row // 2) % 4 - (owner // 2) % 4 + 4) % 4
    dc = (row % 2 - owner % 2 + 2) % 2
    return dz * 8 + dy * 2 + dc


def kernel(
    lists, emb_in, cent_in,
    new_out, near_out,
    rows, cent, stage, back, b0, b1, b2, b3, c0, c1, c2, c3,
    ex, wts, stat, wb, cum, f0, f1, f2, f3, st, bb, rb, mine, ours, asks, info, ours_at, info_at,
    loc_sem, ms, mr, gs, gr, xs, xr, s1, r1, s2, r2, s3, r3, ss, sr, ns, nr, out_sem,
):
    row, ctr = lax.axis_index("row"), lax.axis_index("ctr")
    fetched = (b0, b1, b2, b3)
    landed = (c0, c1, c2, c3)
    fresh = (f0, f1, f2, f3)
    RB = rows.shape[0] // N_CTR
    D = rows.shape[1]
    H = cent.shape[1] // PIECES
    CB = cent.shape[1]
    Q = RB // 4

    emb_copy = pltpu.make_async_copy(emb_in, rows.at[pl.ds(0, RB)], loc_sem.at[0])
    cent_copy = pltpu.make_async_copy(cent_in, cent, loc_sem.at[1])
    emb_copy.start()
    cent_copy.start()

    barrier = pltpu.get_barrier_semaphore()

    def greet(k, carry):
        pl.semaphore_signal(
            barrier, inc=1, device_id=(shifted(row, k, 1), ctr), device_id_type=MESH
        )
        return carry

    lax.fori_loop(1, N_ROW, greet, 0)
    for d in range(1, N_CTR):
        pl.semaphore_signal(
            barrier, inc=1, device_id=(row, lax.rem(ctr + d, N_CTR)), device_id_type=MESH
        )
    pl.semaphore_wait(barrier, N_ROW - 1 + N_CTR - 1)

    lane = lax.broadcasted_iota(jnp.int32, (8, 128), 1)
    line = lax.broadcasted_iota(jnp.int32, (8, 128), 0)
    held = cent.shape[0]
    tile = jnp.where(line == 1, CANDS, jnp.where(line == 0, -1, 0))
    for j in range(CANDS):
        owner, block = lists[0, j] // held, lists[0, j] % held
        tile = jnp.where(jnp.logical_and(line == 0, lane == owner), block, tile)
        tile = jnp.where(jnp.logical_and(line == 1, lane == owner), j, tile)
        tile = jnp.where(jnp.logical_and(line == 2, lane == j), steps_from(owner, row), tile)
    ours[0] = tile
    list_sends = [
        pltpu.make_async_remote_copy(
            src_ref=ours.at[0],
            dst_ref=ours.at[d],
            send_sem=ms.at[d],
            recv_sem=mr.at[d],
            device_id=(row, lax.rem(ctr + d, N_CTR)),
            device_id_type=MESH,
        )
        for d in range(1, N_CTR)
    ]
    for copy in list_sends:
        copy.start()

    right = (row, lax.rem(ctr + 1, N_CTR))
    left = (row, lax.rem(ctr + 3, N_CTR))

    def row_copy(src, dst, part, device, sem):
        return pltpu.make_async_remote_copy(
            src_ref=rows.at[pl.ds(src * RB + part * Q, Q)],
            dst_ref=rows.at[pl.ds(dst * RB + part * Q, Q)],
            send_sem=xs.at[sem],
            recv_sem=xr.at[sem],
            device_id=device,
            device_id_type=MESH,
        )

    to_right = [row_copy(0, 1, part, right, part) for part in range(4)]
    to_left = [row_copy(0, 3, part, left, 4 + part) for part in range(4)]
    onward = [
        row_copy(1, 2, 0, right, 8),
        row_copy(1, 2, 1, right, 9),
        row_copy(3, 2, 2, left, 10),
        row_copy(3, 2, 3, left, 11),
    ]

    def normalise(part):
        def some(t, carry):
            place = pl.ds(pl.multiple_of(part * Q + t * 64, 64), 64)
            values = rows[place, :].astype(jnp.float32)
            scale = lax.rsqrt(jnp.mean(values * values, axis=-1, keepdims=True) + epsilon)
            rows[place, :] = (values * scale).astype(jnp.bfloat16)
            return carry

        lax.fori_loop(0, Q // 64, some, 0)

    def slot_send(src, dst, k, sign, send, recv):
        return pltpu.make_async_remote_copy(
            src_ref=src,
            dst_ref=dst,
            send_sem=send,
            recv_sem=recv,
            device_id=(shifted(row, k, sign), ctr),
            device_id_type=MESH,
        )

    def all_slots(buf_send, buf_recv, send, recv):
        others = pl.ds(1, N_ROW - 1)
        return pltpu.make_async_remote_copy(
            src_ref=buf_send.at[others],
            dst_ref=buf_recv.at[others],
            send_sem=send,
            recv_sem=recv,
            device_id=(row, ctr),
            device_id_type=MESH,
        )

    emb_copy.wait()
    normalise(0)
    to_right[0].start()
    normalise(2)
    to_left[2].start()

    for copy in list_sends:
        copy.wait_recv()
    mine[...] = functools.reduce(jnp.maximum, [ours[d] for d in range(N_CTR)])
    asks[0] = mine[...]

    def ask(t, carry):
        k = t
        slot_send(mine, asks.at[k], k, -1, gs.at[0], gr.at[0]).start()
        return carry

    lax.fori_loop(1, N_ROW, ask, 0)
    ours_copy = pltpu.make_async_copy(ours, ours_at, loc_sem.at[2])
    ours_copy.start()
    normalise(1)
    to_right[1].start()
    normalise(3)
    to_left[3].start()
    for part in (2, 3):
        to_right[part].start()
        to_left[part - 2].start()

    asked = pltpu.make_async_remote_copy(
        src_ref=asks.at[pl.ds(1, N_ROW - 1)],
        dst_ref=asks.at[pl.ds(1, N_ROW - 1)],
        send_sem=gs.at[0],
        recv_sem=gr.at[0],
        device_id=(row, ctr),
        device_id_type=MESH,
    )
    asked.wait_recv()
    shape = (N_ROW, 128)
    slot = lax.broadcasted_iota(jnp.int32, shape, 0)
    column = lax.broadcasted_iota(jnp.int32, shape, 1)
    table = asks[:, 0, :]
    want = jnp.max(jnp.where(column == row, table, -1), axis=1, keepdims=True)
    want = jnp.broadcast_to(want, shape)
    want_row = jnp.max(jnp.where(column == slot, want, -1), axis=0, keepdims=True)
    key = jnp.where(want < 0, held, want) * N_ROW + slot
    key_row = jnp.max(jnp.where(column == slot, key, -1), axis=0, keepdims=True)
    less = jnp.logical_and(key_row < key, column < N_ROW)
    rank = jnp.sum(jnp.where(less, 1, 0), axis=1, keepdims=True)
    at = rank == column
    info[0:1, :] = want_row
    info[1:2, :] = jnp.sum(jnp.where(at, slot, 0), axis=0, keepdims=True)
    this = jnp.sum(jnp.where(at, want, 0), axis=0, keepdims=True)
    before = jnp.sum(jnp.where(rank + 1 == column, want, 0), axis=0, keepdims=True)
    after_first = lax.broadcasted_iota(jnp.int32, (1, 128), 1) > 0
    info[2:3, :] = jnp.where(jnp.logical_and(this == before, after_first), 1, 0)
    info[3:4, :] = jnp.max(jnp.where(want == column, rank, -1), axis=0, keepdims=True)
    info[4:8, :] = jnp.zeros((4, 128), jnp.int32)
    info_copy = pltpu.make_async_copy(info, info_at, loc_sem.at[3])
    info_copy.start()
    info_copy.wait()
    ours_copy.wait()

    cent_copy.wait()
    for i in range(PIECES):

        def fetch(t, carry):
            k = lax.rem(t * 5, N_ROW)
            block = jnp.maximum(info_at[0, k], 0)
            stage[i, k] = cent[block, i * H : (i + 1) * H, :]

            @pl.when(k != 0)
            def _():
                slot_send(stage.at[i, k], fetched[i].at[k], k, 1, s1.at[i], r1.at[i]).start()

            return carry

        lax.fori_loop(0, N_ROW, fetch, 0)
        fetched[i][0] = stage[i, 0]

    to_right[0].wait_recv()
    onward[0].start()
    to_left[2].wait_recv()
    onward[2].start()
    to_right[1].wait_recv()
    onward[1].start()
    to_left[3].wait_recv()
    onward[3].start()
    for i in range(PIECES):
        done = all_slots(stage.at[i], fetched[i], s1.at[i], r1.at[i])
        done.wait_send()
        done.wait_recv()

    def scores_of(s):
        def pick(j, carry):
            slot = ours_at[s, 2, j]
            for i in range(PIECES):
                stat[pl.ds(pl.multiple_of(j * CB + i * H, H), H), :] = fetched[i][slot]
            return carry

        lax.fori_loop(0, CANDS, pick, 0)

        def tile(n, carry):
            place = pl.ds(pl.multiple_of(n * 256, 256), 256)
            near = pl.ds(pl.multiple_of(s * RB + n * 256, 256), 256)
            score = score_scale * lax.dot_general(
                stat[...], rows[near, :], (((1,), (1,)), ((), ())),
                preferred_element_type=jnp.float32,
            )
            top = jnp.max(score, axis=0, keepdims=True)
            power = jnp.exp(score - top)
            ex[s, :, place] = power
            st[0, s : s + 1, place] = top
            st[0, N_CTR + s : N_CTR + s + 1, place] = jnp.sum(power, axis=0, keepdims=True)
            return carry

        lax.fori_loop(0, RB // 256, tile, 0)

    scores_of(0)
    to_right[2].wait_recv()
    to_right[3].wait_recv()
    scores_of(1)
    to_left[0].wait_recv()
    to_left[1].wait_recv()
    scores_of(3)
    for copy in onward:
        copy.wait_recv()
    scores_of(2)
    for copy in to_right + to_left + onward + list_sends:
        copy.wait_send()
    asked.wait_send()

    stat_sends = [
        pltpu.make_async_remote_copy(
            src_ref=st.at[0],
            dst_ref=st.at[d],
            send_sem=ss.at[d],
            recv_sem=sr.at[d],
            device_id=(row, lax.rem(ctr + d, N_CTR)),
            device_id_type=MESH,
        )
        for d in range(1, N_CTR)
    ]
    for copy in stat_sends:
        copy.start()
    for s in range(N_CTR):
        wts[s, CANDS] = jnp.zeros(wts.shape[2:], wts.dtype)
    for copy in stat_sends:
        copy.wait()
    for s in range(N_CTR):
        tops = [st[d, (s - d) % N_CTR : (s - d) % N_CTR + 1, :] for d in range(N_CTR)]
        totals = [
            st[d, N_CTR + (s - d) % N_CTR : N_CTR + (s - d) % N_CTR + 1, :] for d in range(N_CTR)
        ]
        highest = functools.reduce(jnp.maximum, tops)
        total = functools.reduce(
            jnp.add, [total * jnp.exp(top - highest) for top, total in zip(tops, totals)]
        )
        factor = jnp.exp(tops[0] - highest) / total

        def weigh(j, carry):
            place = pl.ds(pl.multiple_of(j * CB, CB), CB)
            wts[s, j] = (ex[s, place, :] * factor).astype(jnp.bfloat16)
            return carry

        lax.fori_loop(0, CANDS, weigh, 0)

    half = N_ROW // 2
    for i in range(PIECES):
        for h in range(2):

            def lay(t, carry):
                owner = shifted(row, h * half + t, -1)
                for s in range(N_CTR):
                    j = ours_at[s, 1, owner]
                    wb[pl.ds(pl.multiple_of(t * H, H), H), s * RB : (s + 1) * RB] = wts[
                        s, j, i * H : (i + 1) * H, :
                    ]
                return carry

            lax.fori_loop(0, half, lay, 0)

            def multiply(n, carry):
                place = pl.ds(pl.multiple_of(n * 256, 256), 256)
                total = jnp.dot(wb[...], rows[:, place], preferred_element_type=jnp.float32)
                stage[i, h * half : (h + 1) * half, :, place] = total.reshape(half, H, 256).astype(
                    jnp.bfloat16
                )
                return carry

            lax.fori_loop(0, D // 256, multiply, 0)

            def deliver(t, carry):
                k = h * half + lax.rem(t * 5, half)

                @pl.when(k != 0)
                def _():
                    slot_send(stage.at[i, k], landed[i].at[k], k, -1, s2.at[i], r2.at[i]).start()

                return carry

            lax.fori_loop(0, half, deliver, 0)
        landed[i][0] = stage[i, 0]

    out_copies = []
    for i in range(PIECES):
        all_slots(stage.at[i], landed[i], s2.at[i], r2.at[i]).wait_recv()

        def add(t, total):
            keep = info_at[2, t].astype(jnp.float32)
            total = landed[i][info_at[1, t]].astype(jnp.float32) + total * keep
            cum[t] = total
            return total

        lax.fori_loop(0, N_ROW, add, jnp.zeros((H, D), jnp.float32))

        def renew(b, carry):
            end = info_at[3, b]
            total = cum[jnp.maximum(end, 0)]
            total = jnp.where(end >= 0, total, jnp.zeros_like(total))
            scale = lax.rsqrt(jnp.mean(total * total, axis=-1, keepdims=True) + epsilon)
            fresh[i][b] = (total * scale * (1.0 / math.sqrt(D))).astype(jnp.bfloat16)
            return carry

        lax.fori_loop(0, cent.shape[0], renew, 0)

        def give(t, carry):
            k = lax.rem(t * 5, N_ROW)
            back[i, k] = fresh[i][jnp.maximum(info_at[0, k], 0)]

            @pl.when(k != 0)
            def _():
                slot_send(back.at[i, k], fetched[i].at[k], k, 1, s3.at[i], r3.at[i]).start()

            return carry

        lax.fori_loop(0, N_ROW, give, 0)
        fetched[i][0] = back[i, 0]
        out = pltpu.make_async_copy(
            fresh[i], new_out.at[:, pl.ds(i * H, H)], out_sem.at[i]
        )
        out.start()
        out_copies.append(out)

    for i in range(PIECES):
        all_slots(back.at[i], fetched[i], s3.at[i], r3.at[i]).wait_recv()
        for s in range(N_CTR):
            for j in range(CANDS):
                stat[j * H : (j + 1) * H, :] = fetched[i][ours_at[s, 2, j]]

            def tile(n, carry):
                place = pl.ds(pl.multiple_of(n * 256, 256), 256)
                near = pl.ds(pl.multiple_of(s * RB + n * 256, 256), 256)
                similar = lax.dot_general(
                    stat[0 : CANDS * H, :], rows[near, :], (((1,), (1,)), ((), ())),
                    preferred_element_type=jnp.float32,
                )
                best = jnp.max(similar, axis=0, keepdims=True)
                if i > 0:
                    best = jnp.maximum(best, bb[s, 0:1, place])
                bb[s, :, place] = jnp.broadcast_to(best, (8, 256))
                return carry

            lax.fori_loop(0, RB // 256, tile, 0)
    best_sends = [
        pltpu.make_async_remote_copy(
            src_ref=bb.at[d],
            dst_ref=rb.at[d],
            send_sem=ns.at[d],
            recv_sem=nr.at[d],
            device_id=(row, lax.rem(ctr - d + N_CTR, N_CTR)),
            device_id_type=MESH,
        )
        for d in range(1, N_CTR)
    ]
    for copy in best_sends:
        copy.start()
    for i in range(PIECES):
        all_slots(stage.at[i], landed[i], s2.at[i], r2.at[i]).wait_send()
        all_slots(back.at[i], fetched[i], s3.at[i], r3.at[i]).wait_send()
        out_copies[i].wait()
    for copy in best_sends:
        copy.wait()
    best = bb[0, 0:1, :]
    for d in range(1, N_CTR):
        best = jnp.maximum(best, rb[d, 0:1, :])
    near_out[...] = best.reshape(near_out.shape)


def on_device(embeddings, centroids, candidates):
    blocks, width, features = centroids.shape
    rb = embeddings.shape[0]
    held = width // PIECES
    bf16, f32 = jnp.bfloat16, jnp.float32
    piece = pltpu.VMEM((N_ROW, held, features), bf16)
    dma = pltpu.SemaphoreType.DMA
    renewed, nearest = pl.pallas_call(
        kernel,
        out_shape=(
            jax.ShapeDtypeStruct(centroids.shape, bf16),
            jax.ShapeDtypeStruct((rb,), f32),
        ),
        in_specs=[pl.BlockSpec(memory_space=pltpu.SMEM)]
        + [pl.BlockSpec(memory_space=pl.ANY)] * 2,
        out_specs=(
            pl.BlockSpec(memory_space=pl.ANY),
            pl.BlockSpec(memory_space=pltpu.VMEM),
        ),
        scratch_shapes=[
            pltpu.VMEM((N_CTR * rb, features), bf16),
            pltpu.VMEM((blocks, width, features), bf16),
            pltpu.VMEM((PIECES, N_ROW, held, features), bf16),
            pltpu.VMEM((PIECES, N_ROW, held, features), bf16),
            *([piece] * 8),
            pltpu.VMEM((N_CTR, CANDS * width, rb), f32),
            pltpu.VMEM((N_CTR, CANDS + 1, width, rb), bf16),
            pltpu.VMEM((CANDS * width, features), bf16),
            pltpu.VMEM((N_ROW // 2 * held, N_CTR * rb), bf16),
            pltpu.VMEM((N_ROW, held, features), f32),
            *([pltpu.VMEM((blocks, held, features), bf16)] * 4),
            pltpu.VMEM((N_CTR, 2 * N_CTR, rb), f32),
            pltpu.VMEM((N_CTR, 8, rb), f32),
            pltpu.VMEM((N_CTR, 8, rb), f32),
            pltpu.VMEM((8, 128), jnp.int32),
            pltpu.VMEM((N_CTR, 8, 128), jnp.int32),
            pltpu.VMEM((N_ROW, 8, 128), jnp.int32),
            pltpu.VMEM((8, 128), jnp.int32),
            pltpu.SMEM((N_CTR, 8, 128), jnp.int32),
            pltpu.SMEM((8, 128), jnp.int32),
            dma((4,)),
            dma((N_CTR,)),
            dma((N_CTR,)),
            dma((1,)),
            dma((1,)),
            dma((12,)),
            dma((12,)),
            *([dma((PIECES,))] * 6),
            *([dma((N_CTR,))] * 4),
            dma((PIECES,)),
        ],
        compiler_params=pltpu.CompilerParams(
            collective_id=0, has_side_effects=True, vmem_limit_bytes=60 * 2**20
        ),
    )(candidates, embeddings, centroids)
    return renewed, nearest


def solution(mesh):
    in_specs = (P(("row", "ctr"), None), P("row", "ctr", None), P(("row", "ctr"), None))
    out_specs = (P("row", "ctr", None), P(("row", "ctr")))
    return jax.shard_map(
        on_device, mesh=mesh, in_specs=in_specs, out_specs=out_specs, check_vma=False
    )
```

```python
import functools
import math

import jax
import jax.numpy as jnp
from jax import lax
from jax.experimental import pallas as pl
from jax.experimental.pallas import tpu as pltpu
from jax.sharding import PartitionSpec as P

score_scale = 1.5
epsilon = 1e-06
MESH = pl.DeviceIdType.MESH

N_Z, N_Y, N_C = 4, 4, 2
N_ROW = N_Z * N_Y * N_C
N_CTR = 4
CANDS = 6
PIECES = 4


def shifted(row, k, sign):
    z, y, c = row // 8, (row // 2) % 4, row % 2
    dz, dy, dc = k // 8, (k // 2) % 4, k % 2
    return (
        lax.rem(z + sign * dz + 4, 4) * 8
        + lax.rem(y + sign * dy + 4, 4) * 2
        + lax.rem(c + sign * dc + 2, 2)
    )


def steps(t):
    return lax.rem(t * 5, N_ROW)


def slot_from(owner, row):
    dz = (row // 8 - owner // 8 + 4) % 4
    dy = ((row // 2) % 4 - (owner // 2) % 4 + 4) % 4
    dc = (row % 2 - owner % 2 + 2) % 2
    return (dz * 8 + dy * 2 + dc) * 13 % N_ROW


def kernel(
    lists, emb_in, cent_in,
    new_out, near_out,
    rows, cent, stage, back, b0, b1, b2, b3, c0, c1, c2, c3,
    ex, part, wts, stat, wb, cum, f0, f1, f2, f3, st, bb, rb, mine, ours, asks, info, ours_at, info_at,
    loc_sem, ms, mr, gs, gr, xs, xr, s1, r1, s2, r2, s3, r3, ss, sr, ns, nr, out_sem,
):
    row, ctr = lax.axis_index("row"), lax.axis_index("ctr")
    fetched = (b0, b1, b2, b3)
    landed = (c0, c1, c2, c3)
    fresh = (f0, f1, f2, f3)
    RB = rows.shape[0] // N_CTR
    D = rows.shape[1]
    H = cent.shape[1] // PIECES
    CB = cent.shape[1]
    PARTS = 6
    Q = RB // PARTS

    emb_copy = pltpu.make_async_copy(emb_in, rows.at[pl.ds(0, RB)], loc_sem.at[0])
    cent_copy = pltpu.make_async_copy(cent_in, cent, loc_sem.at[1])
    emb_copy.start()
    cent_copy.start()

    barrier = pltpu.get_barrier_semaphore()

    def greet(k, carry):
        pl.semaphore_signal(
            barrier, inc=1, device_id=(shifted(row, k, 1), ctr), device_id_type=MESH
        )
        return carry

    lax.fori_loop(1, N_ROW, greet, 0)
    for d in range(1, N_CTR):
        pl.semaphore_signal(
            barrier, inc=1, device_id=(row, lax.rem(ctr + d, N_CTR)), device_id_type=MESH
        )

    lane = lax.broadcasted_iota(jnp.int32, (8, 128), 1)
    line = lax.broadcasted_iota(jnp.int32, (8, 128), 0)
    held = cent.shape[0]
    tile = jnp.where(line == 1, CANDS, jnp.where(line == 0, -1, 0))
    for j in range(CANDS):
        owner, block = lists[0, j] // held, lists[0, j] % held
        tile = jnp.where(jnp.logical_and(line == 0, lane == owner), block, tile)
        tile = jnp.where(jnp.logical_and(line == 1, lane == owner), j, tile)
        tile = jnp.where(jnp.logical_and(line == 2, lane == j), slot_from(owner, row), tile)
    ours[0] = tile
    emb_copy.wait()

    def normalise(t, carry):
        place = pl.ds(pl.multiple_of(t * 64, 64), 64)
        values = rows[place, :].astype(jnp.float32)
        scale = lax.rsqrt(jnp.mean(values * values, axis=-1, keepdims=True) + epsilon)
        rows[place, :] = (values * scale).astype(jnp.bfloat16)
        return carry

    lax.fori_loop(0, RB // 64, normalise, 0)
    pl.semaphore_wait(barrier, N_ROW - 1 + N_CTR - 1)
    list_sends = [
        pltpu.make_async_remote_copy(
            src_ref=ours.at[0],
            dst_ref=ours.at[d],
            send_sem=ms.at[d],
            recv_sem=mr.at[d],
            device_id=(row, lax.rem(ctr + d, N_CTR)),
            device_id_type=MESH,
        )
        for d in range(1, N_CTR)
    ]
    for copy in list_sends:
        copy.start()

    right = (row, lax.rem(ctr + 1, N_CTR))
    left = (row, lax.rem(ctr + 3, N_CTR))

    def row_copy(src, dst, p, device, sem):
        return pltpu.make_async_remote_copy(
            src_ref=rows.at[pl.ds(src * RB + p * Q, Q)],
            dst_ref=rows.at[pl.ds(dst * RB + p * Q, Q)],
            send_sem=xs.at[sem],
            recv_sem=xr.at[sem],
            device_id=device,
            device_id_type=MESH,
        )

    to_right = [row_copy(0, 1, p, right, p) for p in range(PARTS)]
    to_left = [row_copy(0, 3, p, left, PARTS + p) for p in range(PARTS)]
    onward = [row_copy(1, 2, p, right, 2 * PARTS + p) for p in range(PARTS // 2)]
    onward += [row_copy(3, 2, p, left, 2 * PARTS + p) for p in range(PARTS // 2, PARTS)]

    def slot_send(src, dst, k, sign, send, recv):
        return pltpu.make_async_remote_copy(
            src_ref=src,
            dst_ref=dst,
            send_sem=send,
            recv_sem=recv,
            device_id=(shifted(row, steps(k), sign), ctr),
            device_id_type=MESH,
        )

    def all_slots(buf_send, buf_recv, send, recv):
        others = pl.ds(1, N_ROW - 1)
        return pltpu.make_async_remote_copy(
            src_ref=buf_send.at[others],
            dst_ref=buf_recv.at[others],
            send_sem=send,
            recv_sem=recv,
            device_id=(row, ctr),
            device_id_type=MESH,
        )

    for p in range(2):
        to_right[p].start()
        to_left[PARTS - 1 - p].start()

    for copy in list_sends:
        copy.wait_recv()
    mine[...] = functools.reduce(jnp.maximum, [ours[d] for d in range(N_CTR)])
    asks[0] = mine[...]

    def ask(t, carry):
        k = t
        slot_send(mine, asks.at[k], k, -1, gs.at[0], gr.at[0]).start()
        return carry

    lax.fori_loop(1, N_ROW, ask, 0)
    ours_copy = pltpu.make_async_copy(ours, ours_at, loc_sem.at[2])
    ours_copy.start()
    for p in range(2, PARTS):
        to_right[p].start()
        to_left[PARTS - 1 - p].start()

    asked = pltpu.make_async_remote_copy(
        src_ref=asks.at[pl.ds(1, N_ROW - 1)],
        dst_ref=asks.at[pl.ds(1, N_ROW - 1)],
        send_sem=gs.at[0],
        recv_sem=gr.at[0],
        device_id=(row, ctr),
        device_id_type=MESH,
    )
    asked.wait_recv()
    shape = (N_ROW, 128)
    slot = lax.broadcasted_iota(jnp.int32, shape, 0)
    column = lax.broadcasted_iota(jnp.int32, shape, 1)
    table = asks[:, 0, :]
    want = jnp.max(jnp.where(column == row, table, -1), axis=1, keepdims=True)
    want = jnp.broadcast_to(want, shape)
    want_row = jnp.max(jnp.where(column == slot, want, -1), axis=0, keepdims=True)
    key = jnp.where(want < 0, held, want) * N_ROW + slot
    key_row = jnp.max(jnp.where(column == slot, key, -1), axis=0, keepdims=True)
    less = jnp.logical_and(key_row < key, column < N_ROW)
    rank = jnp.sum(jnp.where(less, 1, 0), axis=1, keepdims=True)
    at = rank == column
    info[0:1, :] = want_row
    info[1:2, :] = jnp.sum(jnp.where(at, slot, 0), axis=0, keepdims=True)
    this = jnp.sum(jnp.where(at, want, 0), axis=0, keepdims=True)
    before = jnp.sum(jnp.where(rank + 1 == column, want, 0), axis=0, keepdims=True)
    after_first = lax.broadcasted_iota(jnp.int32, (1, 128), 1) > 0
    info[2:3, :] = jnp.where(jnp.logical_and(this == before, after_first), 1, 0)
    info[3:4, :] = jnp.max(jnp.where(want == column, rank, -1), axis=0, keepdims=True)
    info[4:8, :] = jnp.zeros((4, 128), jnp.int32)
    info_copy = pltpu.make_async_copy(info, info_at, loc_sem.at[3])
    info_copy.start()
    info_copy.wait()
    ours_copy.wait()

    cent_copy.wait()
    for i in range(PIECES):

        def fetch(t, carry):
            k = t
            block = jnp.maximum(info_at[0, k], 0)
            stage[i, k] = cent[block, i * H : (i + 1) * H, :]

            @pl.when(k != 0)
            def _():
                slot_send(stage.at[i, k], fetched[i].at[k], k, 1, s1.at[i], r1.at[i]).start()

            return carry

        lax.fori_loop(0, N_ROW, fetch, 0)
        fetched[i][0] = stage[i, 0]

    for p in range(PARTS // 2):
        to_right[p].wait_recv()
        onward[p].start()
        to_left[PARTS - 1 - p].wait_recv()
        onward[PARTS - 1 - p].start()
    for p in range(PARTS // 2):
        to_right[PARTS // 2 + p].wait_recv()
        to_left[p].wait_recv()

    AHEAD = PIECES - 1
    G = CANDS * H

    def scores_of(s, first, tiles):
        lo, hi = (0, AHEAD) if first else (AHEAD, PIECES)
        line = 0 if first else 2 * N_CTR

        def pick(j, carry):
            slot = ours_at[s, 2, j]
            for i in range(lo, hi):
                stat[pl.ds(pl.multiple_of(i * G + j * H, H), H), :] = fetched[i][slot]
            return carry

        lax.fori_loop(0, CANDS, pick, 0)

        def tile(n, carry):
            place = pl.ds(pl.multiple_of(n * 256, 256), 256)
            near = pl.ds(pl.multiple_of(s * RB + n * 256, 256), 256)
            score = score_scale * lax.dot_general(
                stat[lo * G : hi * G, :], rows[near, :], (((1,), (1,)), ((), ())),
                preferred_element_type=jnp.float32,
            )
            top = jnp.max(score, axis=0, keepdims=True)
            power = jnp.exp(score - top)
            ex[s, lo:hi, :, place] = power.reshape(hi - lo, G, 256)
            part[line + s : line + s + 1, place] = top
            part[line + N_CTR + s : line + N_CTR + s + 1, place] = jnp.sum(
                power, axis=0, keepdims=True
            )
            return carry

        if len(tiles) == 1:
            tile(tiles[0], 0)
        else:
            step = tiles[1] - tiles[0]
            lax.fori_loop(0, len(tiles), lambda t, c: tile(tiles[0] + t * step, c), 0)

    def fetch_done(i):
        done = all_slots(stage.at[i], fetched[i], s1.at[i], r1.at[i])
        done.wait_send()
        done.wait_recv()

    whole = range(RB // 256)
    for i in range(AHEAD):
        fetch_done(i)
    for s in (0, 1, 3):
        scores_of(s, True, whole)
    for p in (0, 1, 4, 5):
        onward[p].wait_recv()
    scores_of(2, True, (0, 2))
    fetch_done(AHEAD)
    for s in (0, 1, 3):
        scores_of(s, False, whole)
    scores_of(2, False, (0, 2))
    for p in (2, 3):
        onward[p].wait_recv()
    scores_of(2, True, (1,))
    scores_of(2, False, (1,))
    for copy in to_right + to_left + onward + list_sends:
        copy.wait_send()
    asked.wait_send()

    top_a, top_b = part[0:N_CTR, :], part[2 * N_CTR : 3 * N_CTR, :]
    top = jnp.maximum(top_a, top_b)
    st[0, 0:N_CTR, :] = top
    st[0, N_CTR : 2 * N_CTR, :] = part[N_CTR : 2 * N_CTR, :] * jnp.exp(top_a - top) + part[
        3 * N_CTR : 4 * N_CTR, :
    ] * jnp.exp(top_b - top)

    stat_sends = [
        pltpu.make_async_remote_copy(
            src_ref=st.at[0],
            dst_ref=st.at[d],
            send_sem=ss.at[d],
            recv_sem=sr.at[d],
            device_id=(row, lax.rem(ctr + d, N_CTR)),
            device_id_type=MESH,
        )
        for d in range(1, N_CTR)
    ]
    for copy in stat_sends:
        copy.start()
    for s in range(N_CTR):
        wts[s, CANDS] = jnp.zeros(wts.shape[2:], wts.dtype)
    for copy in stat_sends:
        copy.wait()
    for s in range(N_CTR):
        tops = [st[d, (s - d) % N_CTR : (s - d) % N_CTR + 1, :] for d in range(N_CTR)]
        totals = [
            st[d, N_CTR + (s - d) % N_CTR : N_CTR + (s - d) % N_CTR + 1, :] for d in range(N_CTR)
        ]
        highest = functools.reduce(jnp.maximum, tops)
        total = functools.reduce(
            jnp.add, [total * jnp.exp(top - highest) for top, total in zip(tops, totals)]
        )
        for line in (0, 2 * N_CTR):
            part[line + N_CTR + s : line + N_CTR + s + 1, :] = (
                jnp.exp(part[line + s : line + s + 1, :] - highest) / total
            )

    for i in range(PIECES):
        line = N_CTR if i < AHEAD else 3 * N_CTR
        for s in range(N_CTR):
            factor = part[line + s : line + s + 1, :]

            def weigh(j, carry):
                place = pl.ds(pl.multiple_of(j * H, H), H)
                wts[s, j] = (ex[s, i, place, :] * factor).astype(jnp.bfloat16)
                return carry

            lax.fori_loop(0, CANDS, weigh, 0)
        batch = N_ROW // 4 if i == 0 else N_ROW // 2
        for h in range(N_ROW // batch):

            def lay(t, carry):
                owner = shifted(row, steps(h * batch + t), -1)
                for s in range(N_CTR):
                    j = ours_at[s, 1, owner]
                    wb[pl.ds(pl.multiple_of(t * H, H), H), s * RB : (s + 1) * RB] = wts[s, j]
                return carry

            lax.fori_loop(0, batch, lay, 0)

            def multiply(n, carry):
                place = pl.ds(pl.multiple_of(n * 256, 256), 256)
                total = jnp.dot(
                    wb[0 : batch * H, :], rows[:, place], preferred_element_type=jnp.float32
                )
                stage[i, h * batch : (h + 1) * batch, :, place] = total.reshape(
                    batch, H, 256
                ).astype(jnp.bfloat16)
                return carry

            lax.fori_loop(0, D // 256, multiply, 0)

            def deliver(t, carry):
                k = h * batch + t

                @pl.when(k != 0)
                def _():
                    slot_send(stage.at[i, k], landed[i].at[k], k, -1, s2.at[i], r2.at[i]).start()

                return carry

            lax.fori_loop(0, batch, deliver, 0)
        landed[i][0] = stage[i, 0]

    out_copies = []
    for i in range(PIECES):
        all_slots(stage.at[i], landed[i], s2.at[i], r2.at[i]).wait_recv()

        def add(t, total):
            keep = info_at[2, t].astype(jnp.float32)
            total = landed[i][info_at[1, t]].astype(jnp.float32) + total * keep
            cum[t] = total
            return total

        lax.fori_loop(0, N_ROW, add, jnp.zeros((H, D), jnp.float32))

        def renew(b, carry):
            end = info_at[3, b]
            total = cum[jnp.maximum(end, 0)]
            total = jnp.where(end >= 0, total, jnp.zeros_like(total))
            scale = lax.rsqrt(jnp.mean(total * total, axis=-1, keepdims=True) + epsilon)
            fresh[i][b] = (total * scale * (1.0 / math.sqrt(D))).astype(jnp.bfloat16)
            return carry

        lax.fori_loop(0, cent.shape[0], renew, 0)

        def give(t, carry):
            k = t
            back[i, k] = fresh[i][jnp.maximum(info_at[0, k], 0)]

            @pl.when(k != 0)
            def _():
                slot_send(back.at[i, k], fetched[i].at[k], k, 1, s3.at[i], r3.at[i]).start()

            return carry

        lax.fori_loop(0, N_ROW, give, 0)
        fetched[i][0] = back[i, 0]
        out = pltpu.make_async_copy(
            fresh[i], new_out.at[:, pl.ds(i * H, H)], out_sem.at[i]
        )
        out.start()
        out_copies.append(out)

    for i in range(PIECES):
        all_slots(back.at[i], fetched[i], s3.at[i], r3.at[i]).wait_recv()
        for s in range(N_CTR):
            for j in range(CANDS):
                stat[j * H : (j + 1) * H, :] = fetched[i][ours_at[s, 2, j]]

            def tile(n, carry):
                place = pl.ds(pl.multiple_of(n * 256, 256), 256)
                near = pl.ds(pl.multiple_of(s * RB + n * 256, 256), 256)
                similar = lax.dot_general(
                    stat[0 : CANDS * H, :], rows[near, :], (((1,), (1,)), ((), ())),
                    preferred_element_type=jnp.float32,
                )
                best = jnp.max(similar, axis=0, keepdims=True)
                if i > 0:
                    best = jnp.maximum(best, bb[s, 0:1, place])
                bb[s, :, place] = jnp.broadcast_to(best, (8, 256))
                return carry

            lax.fori_loop(0, RB // 256, tile, 0)
    best_sends = [
        pltpu.make_async_remote_copy(
            src_ref=bb.at[d],
            dst_ref=rb.at[d],
            send_sem=ns.at[d],
            recv_sem=nr.at[d],
            device_id=(row, lax.rem(ctr - d + N_CTR, N_CTR)),
            device_id_type=MESH,
        )
        for d in range(1, N_CTR)
    ]
    for copy in best_sends:
        copy.start()
    for i in range(PIECES):
        all_slots(stage.at[i], landed[i], s2.at[i], r2.at[i]).wait_send()
        all_slots(back.at[i], fetched[i], s3.at[i], r3.at[i]).wait_send()
        out_copies[i].wait()
    for copy in best_sends:
        copy.wait()
    best = bb[0, 0:1, :]
    for d in range(1, N_CTR):
        best = jnp.maximum(best, rb[d, 0:1, :])
    near_out[...] = best.reshape(near_out.shape)


def on_device(embeddings, centroids, candidates):
    blocks, width, features = centroids.shape
    rb = embeddings.shape[0]
    held = width // PIECES
    bf16, f32 = jnp.bfloat16, jnp.float32
    piece = pltpu.VMEM((N_ROW, held, features), bf16)
    dma = pltpu.SemaphoreType.DMA
    renewed, nearest = pl.pallas_call(
        kernel,
        out_shape=(
            jax.ShapeDtypeStruct(centroids.shape, bf16),
            jax.ShapeDtypeStruct((rb,), f32),
        ),
        in_specs=[pl.BlockSpec(memory_space=pltpu.SMEM)]
        + [pl.BlockSpec(memory_space=pl.ANY)] * 2,
        out_specs=(
            pl.BlockSpec(memory_space=pl.ANY),
            pl.BlockSpec(memory_space=pltpu.VMEM),
        ),
        scratch_shapes=[
            pltpu.VMEM((N_CTR * rb, features), bf16),
            pltpu.VMEM((blocks, width, features), bf16),
            pltpu.VMEM((PIECES, N_ROW, held, features), bf16),
            pltpu.VMEM((PIECES, N_ROW, held, features), bf16),
            *([piece] * 8),
            pltpu.VMEM((N_CTR, PIECES, CANDS * held, rb), f32),
            pltpu.VMEM((4 * N_CTR, rb), f32),
            pltpu.VMEM((N_CTR, CANDS + 1, held, rb), bf16),
            pltpu.VMEM((CANDS * width, features), bf16),
            pltpu.VMEM((N_ROW // 2 * held, N_CTR * rb), bf16),
            pltpu.VMEM((N_ROW, held, features), f32),
            *([pltpu.VMEM((blocks, held, features), bf16)] * 4),
            pltpu.VMEM((N_CTR, 2 * N_CTR, rb), f32),
            pltpu.VMEM((N_CTR, 8, rb), f32),
            pltpu.VMEM((N_CTR, 8, rb), f32),
            pltpu.VMEM((8, 128), jnp.int32),
            pltpu.VMEM((N_CTR, 8, 128), jnp.int32),
            pltpu.VMEM((N_ROW, 8, 128), jnp.int32),
            pltpu.VMEM((8, 128), jnp.int32),
            pltpu.SMEM((N_CTR, 8, 128), jnp.int32),
            pltpu.SMEM((8, 128), jnp.int32),
            dma((4,)),
            dma((N_CTR,)),
            dma((N_CTR,)),
            dma((1,)),
            dma((1,)),
            dma((18,)),
            dma((18,)),
            *([dma((PIECES,))] * 6),
            *([dma((N_CTR,))] * 4),
            dma((PIECES,)),
        ],
        compiler_params=pltpu.CompilerParams(
            collective_id=0, has_side_effects=True, vmem_limit_bytes=60 * 2**20
        ),
    )(candidates, embeddings, centroids)
    return renewed, nearest


def solution(mesh):
    in_specs = (P(("row", "ctr"), None), P("row", "ctr", None), P(("row", "ctr"), None))
    out_specs = (P("row", "ctr", None), P(("row", "ctr")))
    return jax.shard_map(
        on_device, mesh=mesh, in_specs=in_specs, out_specs=out_specs, check_vma=False
    )
```

```python
import functools
import math

import jax
import jax.numpy as jnp
from jax import lax
from jax.experimental import pallas as pl
from jax.experimental.pallas import tpu as pltpu
from jax.sharding import PartitionSpec as P

score_scale = 1.5
epsilon = 1e-06
MESH = pl.DeviceIdType.MESH

N_Z, N_Y, N_C = 4, 4, 2
N_ROW = N_Z * N_Y * N_C
N_CTR = 4
CANDS = 6
PIECES = 4


def shifted(row, k, sign):
    z, y, c = row // 8, (row // 2) % 4, row % 2
    dz, dy, dc = k // 8, (k // 2) % 4, k % 2
    return (
        lax.rem(z + sign * dz + 4, 4) * 8
        + lax.rem(y + sign * dy + 4, 4) * 2
        + lax.rem(c + sign * dc + 2, 2)
    )


def steps(t):
    return lax.rem(t * 5, N_ROW)


def slot_from(owner, row):
    dz = (row // 8 - owner // 8 + 4) % 4
    dy = ((row // 2) % 4 - (owner // 2) % 4 + 4) % 4
    dc = (row % 2 - owner % 2 + 2) % 2
    return (dz * 8 + dy * 2 + dc) * 13 % N_ROW


def kernel(
    lists, emb_in, cent_in,
    new_out, near_out,
    rows, cent, stage, back, b0, b1, b2, b3, c0, c1, c2, c3,
    ex, part, wts, stat, wb, cum, f0, f1, f2, f3, st, bb, rb, mine, ours, asks, info, ours_at, info_at,
    loc_sem, ms, mr, gs, gr, xs, xr, s1, r1, s2, r2, s3, r3, ss, sr, ns, nr, out_sem,
):
    row, ctr = lax.axis_index("row"), lax.axis_index("ctr")
    fetched = (b0, b1, b2, b3)
    landed = (c0, c1, c2, c3)
    fresh = (f0, f1, f2, f3)
    RB = rows.shape[0] // N_CTR
    D = rows.shape[1]
    H = cent.shape[1] // PIECES
    CB = cent.shape[1]
    PARTS = 6
    WIDE = D // 2
    Q = RB // PARTS

    emb_copy = pltpu.make_async_copy(emb_in, rows.at[pl.ds(0, RB)], loc_sem.at[0])
    cent_copy = pltpu.make_async_copy(cent_in, cent, loc_sem.at[1])
    emb_copy.start()
    cent_copy.start()

    barrier = pltpu.get_barrier_semaphore()

    z, y, c = row // 8, (row // 2) % 4, row % 2
    z_at = [lax.rem(z + d, 4) * 8 for d in range(4)]
    y_at = [lax.rem(y + d, 4) * 2 for d in range(4)]
    c_at = [lax.rem(c + d, 2) for d in range(2)]

    def ahead(k):
        return z_at[k // 8] + y_at[(k // 2) % 4] + c_at[k % 2]

    for k in range(1, N_ROW):
        pl.semaphore_signal(barrier, inc=1, device_id=(ahead(k), ctr), device_id_type=MESH)
    for d in range(1, N_CTR):
        pl.semaphore_signal(
            barrier, inc=1, device_id=(row, lax.rem(ctr + d, N_CTR)), device_id_type=MESH
        )

    lane = lax.broadcasted_iota(jnp.int32, (8, 128), 1)
    line = lax.broadcasted_iota(jnp.int32, (8, 128), 0)
    held = cent.shape[0]
    tile = jnp.where(line == 1, CANDS, jnp.where(line == 0, -1, 0))
    for j in range(CANDS):
        owner, block = lists[0, j] // held, lists[0, j] % held
        tile = jnp.where(jnp.logical_and(line == 0, lane == owner), block, tile)
        tile = jnp.where(jnp.logical_and(line == 1, lane == owner), j, tile)
        tile = jnp.where(jnp.logical_and(line == 2, lane == j), slot_from(owner, row), tile)
    ours[0] = tile
    emb_copy.wait()

    def normalise(t, carry):
        place = pl.ds(pl.multiple_of(t * 64, 64), 64)
        values = rows[place, :].astype(jnp.float32)
        scale = lax.rsqrt(jnp.mean(values * values, axis=-1, keepdims=True) + epsilon)
        rows[place, :] = (values * scale).astype(jnp.bfloat16)
        return carry

    lax.fori_loop(0, RB // 64, normalise, 0)
    pl.semaphore_wait(barrier, N_ROW - 1 + N_CTR - 1)
    list_sends = [
        pltpu.make_async_remote_copy(
            src_ref=ours.at[0],
            dst_ref=ours.at[d],
            send_sem=ms.at[d],
            recv_sem=mr.at[d],
            device_id=(row, lax.rem(ctr + d, N_CTR)),
            device_id_type=MESH,
        )
        for d in range(1, N_CTR)
    ]
    for copy in list_sends:
        copy.start()

    right = (row, lax.rem(ctr + 1, N_CTR))
    left = (row, lax.rem(ctr + 3, N_CTR))

    def row_copy(src, dst, p, device, sem):
        return pltpu.make_async_remote_copy(
            src_ref=rows.at[pl.ds(src * RB + p * Q, Q)],
            dst_ref=rows.at[pl.ds(dst * RB + p * Q, Q)],
            send_sem=xs.at[sem],
            recv_sem=xr.at[sem],
            device_id=device,
            device_id_type=MESH,
        )

    to_right = [row_copy(0, 1, p, right, p) for p in range(PARTS)]
    to_left = [row_copy(0, 3, p, left, PARTS + p) for p in range(PARTS)]
    onward = [row_copy(1, 2, p, right, 2 * PARTS + p) for p in range(PARTS // 2)]
    onward += [row_copy(3, 2, p, left, 2 * PARTS + p) for p in range(PARTS // 2, PARTS)]

    def slot_send(src, dst, k, sign, send, recv):
        return pltpu.make_async_remote_copy(
            src_ref=src,
            dst_ref=dst,
            send_sem=send,
            recv_sem=recv,
            device_id=(shifted(row, steps(k), sign), ctr),
            device_id_type=MESH,
        )

    def all_slots(buf_send, buf_recv, send, recv):
        others = pl.ds(1, N_ROW - 1)
        return pltpu.make_async_remote_copy(
            src_ref=buf_send.at[others],
            dst_ref=buf_recv.at[others],
            send_sem=send,
            recv_sem=recv,
            device_id=(row, ctr),
            device_id_type=MESH,
        )

    for p in range(2):
        to_right[p].start()
        to_left[PARTS - 1 - p].start()

    for copy in list_sends:
        copy.wait_recv()
    mine[...] = functools.reduce(jnp.maximum, [ours[d] for d in range(N_CTR)])
    asks[0] = mine[...]

    for t in range(1, N_ROW):
        k = t * 5 % N_ROW
        back_k = (4 - k // 8) % 4 * 8 + (4 - (k // 2) % 4) % 4 * 2 + k % 2
        pltpu.make_async_remote_copy(
            src_ref=mine,
            dst_ref=asks.at[t],
            send_sem=gs.at[0],
            recv_sem=gr.at[0],
            device_id=(ahead(back_k), ctr),
            device_id_type=MESH,
        ).start()
    ours_copy = pltpu.make_async_copy(ours, ours_at, loc_sem.at[2])
    ours_copy.start()
    for p in range(2, PARTS):
        to_right[p].start()
        to_left[PARTS - 1 - p].start()

    asked = pltpu.make_async_remote_copy(
        src_ref=asks.at[pl.ds(1, N_ROW - 1)],
        dst_ref=asks.at[pl.ds(1, N_ROW - 1)],
        send_sem=gs.at[0],
        recv_sem=gr.at[0],
        device_id=(row, ctr),
        device_id_type=MESH,
    )
    asked.wait_recv()
    shape = (N_ROW, 128)
    slot = lax.broadcasted_iota(jnp.int32, shape, 0)
    column = lax.broadcasted_iota(jnp.int32, shape, 1)
    table = asks[:, 0, :]
    want = jnp.max(jnp.where(column == row, table, -1), axis=1, keepdims=True)
    want = jnp.broadcast_to(want, shape)
    want_row = jnp.max(jnp.where(column == slot, want, -1), axis=0, keepdims=True)
    key = jnp.where(want < 0, held, want) * N_ROW + slot
    key_row = jnp.max(jnp.where(column == slot, key, -1), axis=0, keepdims=True)
    less = jnp.logical_and(key_row < key, column < N_ROW)
    rank = jnp.sum(jnp.where(less, 1, 0), axis=1, keepdims=True)
    at = rank == column
    info[0:1, :] = want_row
    info[1:2, :] = jnp.sum(jnp.where(at, slot, 0), axis=0, keepdims=True)
    this = jnp.sum(jnp.where(at, want, 0), axis=0, keepdims=True)
    before = jnp.sum(jnp.where(rank + 1 == column, want, 0), axis=0, keepdims=True)
    after_first = lax.broadcasted_iota(jnp.int32, (1, 128), 1) > 0
    info[2:3, :] = jnp.where(jnp.logical_and(this == before, after_first), 1, 0)
    info[3:4, :] = jnp.max(jnp.where(want == column, rank, -1), axis=0, keepdims=True)
    info[4:8, :] = jnp.zeros((4, 128), jnp.int32)
    info_copy = pltpu.make_async_copy(info, info_at, loc_sem.at[3])
    info_copy.start()
    info_copy.wait()
    ours_copy.wait()

    cent_copy.wait()
    for i in range(PIECES):

        def fetch(t, carry):
            k = t
            block = jnp.maximum(info_at[0, k], 0)
            stage[i, k] = cent[block, i * H : (i + 1) * H, :]

            @pl.when(k != 0)
            def _():
                slot_send(stage.at[i, k], fetched[i].at[k], k, 1, s1.at[i], r1.at[i]).start()

            return carry

        lax.fori_loop(0, N_ROW, fetch, 0)
        fetched[i][0] = stage[i, 0]

    for p in range(PARTS // 2):
        to_right[p].wait_recv()
        onward[p].start()
        to_left[PARTS - 1 - p].wait_recv()
        onward[PARTS - 1 - p].start()
    for p in range(PARTS // 2):
        to_right[PARTS // 2 + p].wait_recv()
        to_left[p].wait_recv()

    AHEAD = PIECES - 1
    G = CANDS * H

    def scores_of(s, first, spans):
        lo, hi = (0, AHEAD) if first else (AHEAD, PIECES)
        line = 0 if first else 2 * N_CTR

        def pick(j, carry):
            slot = ours_at[s, 2, j]
            for i in range(lo, hi):
                stat[pl.ds(pl.multiple_of(i * G + j * H, H), H), :] = fetched[i][slot]
            return carry

        lax.fori_loop(0, CANDS, pick, 0)

        for start, width in spans:
            place = pl.ds(start, width)
            score = score_scale * lax.dot_general(
                stat[lo * G : hi * G, :], rows[pl.ds(s * RB + start, width), :],
                (((1,), (1,)), ((), ())), preferred_element_type=jnp.float32,
            )
            top = jnp.max(score, axis=0, keepdims=True)
            power = jnp.exp(score - top)
            ex[s, lo:hi, :, place] = power.reshape(hi - lo, G, width)
            part[line + s : line + s + 1, place] = top
            part[line + N_CTR + s : line + N_CTR + s + 1, place] = jnp.sum(
                power, axis=0, keepdims=True
            )

    def fetch_done(i):
        done = all_slots(stage.at[i], fetched[i], s1.at[i], r1.at[i])
        done.wait_send()
        done.wait_recv()

    third = RB // 3
    whole = [(0, RB)]
    outer, middle = [(0, third), (2 * third, third)], [(third, third)]
    for i in range(AHEAD):
        fetch_done(i)
    for s in (0, 1, 3):
        scores_of(s, True, whole)
    for p in (0, 1, 4, 5):
        onward[p].wait_recv()
    scores_of(2, True, outer)
    fetch_done(AHEAD)
    for s in (0, 1, 3):
        scores_of(s, False, whole)
    scores_of(2, False, outer)
    for p in (2, 3):
        onward[p].wait_recv()
    scores_of(2, True, middle)
    scores_of(2, False, middle)
    for copy in to_right + to_left + onward + list_sends:
        copy.wait_send()
    asked.wait_send()

    top_a, top_b = part[0:N_CTR, :], part[2 * N_CTR : 3 * N_CTR, :]
    top = jnp.maximum(top_a, top_b)
    st[0, 0:N_CTR, :] = top
    st[0, N_CTR : 2 * N_CTR, :] = part[N_CTR : 2 * N_CTR, :] * jnp.exp(top_a - top) + part[
        3 * N_CTR : 4 * N_CTR, :
    ] * jnp.exp(top_b - top)

    stat_sends = [
        pltpu.make_async_remote_copy(
            src_ref=st.at[0],
            dst_ref=st.at[d],
            send_sem=ss.at[d],
            recv_sem=sr.at[d],
            device_id=(row, lax.rem(ctr + d, N_CTR)),
            device_id_type=MESH,
        )
        for d in range(1, N_CTR)
    ]
    for copy in stat_sends:
        copy.start()
    for s in range(N_CTR):
        wts[s, CANDS] = jnp.zeros(wts.shape[2:], wts.dtype)
    for copy in stat_sends:
        copy.wait()
    for s in range(N_CTR):
        tops = [st[d, (s - d) % N_CTR : (s - d) % N_CTR + 1, :] for d in range(N_CTR)]
        totals = [
            st[d, N_CTR + (s - d) % N_CTR : N_CTR + (s - d) % N_CTR + 1, :] for d in range(N_CTR)
        ]
        highest = functools.reduce(jnp.maximum, tops)
        total = functools.reduce(
            jnp.add, [total * jnp.exp(top - highest) for top, total in zip(tops, totals)]
        )
        for line in (0, 2 * N_CTR):
            part[line + N_CTR + s : line + N_CTR + s + 1, :] = (
                jnp.exp(part[line + s : line + s + 1, :] - highest) / total
            )

    for i in range(PIECES):
        line = N_CTR if i < AHEAD else 3 * N_CTR
        for s in range(N_CTR):
            factor = part[line + s : line + s + 1, :]

            def weigh(j, carry):
                place = pl.ds(pl.multiple_of(j * H, H), H)
                wts[s, j] = (ex[s, i, place, :] * factor).astype(jnp.bfloat16)
                return carry

            lax.fori_loop(0, CANDS, weigh, 0)
        batch = N_ROW // 4 if i == 0 else N_ROW // 2
        for h in range(N_ROW // batch):

            def lay(t, carry):
                owner = shifted(row, steps(h * batch + t), -1)
                for s in range(N_CTR):
                    j = ours_at[s, 1, owner]
                    wb[pl.ds(pl.multiple_of(t * H, H), H), s * RB : (s + 1) * RB] = wts[s, j]
                return carry

            lax.fori_loop(0, batch, lay, 0)

            def multiply(n, carry):
                place = pl.ds(pl.multiple_of(n * WIDE, WIDE), WIDE)
                total = jnp.dot(
                    wb[0 : batch * H, :], rows[:, place], preferred_element_type=jnp.float32
                )
                stage[i, h * batch : (h + 1) * batch, :, place] = total.reshape(
                    batch, H, WIDE
                ).astype(jnp.bfloat16)
                return carry

            lax.fori_loop(0, D // WIDE, multiply, 0)

            def deliver(t, carry):
                k = h * batch + t

                @pl.when(k != 0)
                def _():
                    slot_send(stage.at[i, k], landed[i].at[k], k, -1, s2.at[i], r2.at[i]).start()

                return carry

            lax.fori_loop(0, batch, deliver, 0)
        landed[i][0] = stage[i, 0]

    out_copies = []
    for i in range(PIECES):
        all_slots(stage.at[i], landed[i], s2.at[i], r2.at[i]).wait_recv()

        def add(t, total):
            keep = info_at[2, t].astype(jnp.float32)
            total = landed[i][info_at[1, t]].astype(jnp.float32) + total * keep
            cum[t] = total
            return total

        lax.fori_loop(0, N_ROW, add, jnp.zeros((H, D), jnp.float32))

        def renew(b, carry):
            end = info_at[3, b]
            total = cum[jnp.maximum(end, 0)]
            total = jnp.where(end >= 0, total, jnp.zeros_like(total))
            scale = lax.rsqrt(jnp.mean(total * total, axis=-1, keepdims=True) + epsilon)
            fresh[i][b] = (total * scale * (1.0 / math.sqrt(D))).astype(jnp.bfloat16)
            return carry

        lax.fori_loop(0, cent.shape[0], renew, 0)

        def give(t, carry):
            k = t
            back[i, k] = fresh[i][jnp.maximum(info_at[0, k], 0)]

            @pl.when(k != 0)
            def _():
                slot_send(back.at[i, k], fetched[i].at[k], k, 1, s3.at[i], r3.at[i]).start()

            return carry

        lax.fori_loop(0, N_ROW, give, 0)
        fetched[i][0] = back[i, 0]
        out = pltpu.make_async_copy(
            fresh[i], new_out.at[:, pl.ds(i * H, H)], out_sem.at[i]
        )
        out.start()
        out_copies.append(out)

    for i in range(PIECES):
        all_slots(back.at[i], fetched[i], s3.at[i], r3.at[i]).wait_recv()
        for s in range(N_CTR):
            for j in range(CANDS):
                stat[j * H : (j + 1) * H, :] = fetched[i][ours_at[s, 2, j]]

            similar = lax.dot_general(
                stat[0 : CANDS * H, :], rows[s * RB : (s + 1) * RB, :], (((1,), (1,)), ((), ())),
                preferred_element_type=jnp.float32,
            )
            best = jnp.max(similar, axis=0, keepdims=True)
            if i > 0:
                best = jnp.maximum(best, bb[s, 0:1, :])
            bb[s] = jnp.broadcast_to(best, bb.shape[1:])
    best_sends = [
        pltpu.make_async_remote_copy(
            src_ref=bb.at[d],
            dst_ref=rb.at[d],
            send_sem=ns.at[d],
            recv_sem=nr.at[d],
            device_id=(row, lax.rem(ctr - d + N_CTR, N_CTR)),
            device_id_type=MESH,
        )
        for d in range(1, N_CTR)
    ]
    for copy in best_sends:
        copy.start()
    for i in range(PIECES):
        all_slots(stage.at[i], landed[i], s2.at[i], r2.at[i]).wait_send()
        all_slots(back.at[i], fetched[i], s3.at[i], r3.at[i]).wait_send()
        out_copies[i].wait()
    for copy in best_sends:
        copy.wait()
    best = bb[0, 0:1, :]
    for d in range(1, N_CTR):
        best = jnp.maximum(best, rb[d, 0:1, :])
    near_out[...] = best.reshape(near_out.shape)


def hand_over(renewed, nearest, new_out, near_out, hold, near_hold, sems, outs):
    blocks = renewed.shape[0]
    ins = [pltpu.make_async_copy(renewed.at[b], hold.at[b], sems.at[b]) for b in range(blocks)]
    ins.append(pltpu.make_async_copy(nearest, near_hold, sems.at[blocks]))
    away = [pltpu.make_async_copy(hold.at[b], new_out.at[b], outs.at[b]) for b in range(blocks)]
    away.append(pltpu.make_async_copy(near_hold, near_out, outs.at[blocks]))
    for copy in ins:
        copy.start()
    for one, two in zip(ins, away):
        one.wait()
        two.start()
    for copy in away:
        copy.wait()


def on_device(embeddings, centroids, candidates):
    blocks, width, features = centroids.shape
    rb = embeddings.shape[0]
    held = width // PIECES
    bf16, f32 = jnp.bfloat16, jnp.float32
    piece = pltpu.VMEM((N_ROW, held, features), bf16)
    dma = pltpu.SemaphoreType.DMA
    renewed, nearest = pl.pallas_call(
        kernel,
        out_shape=(
            jax.ShapeDtypeStruct(centroids.shape, bf16),
            jax.ShapeDtypeStruct((rb,), f32),
        ),
        in_specs=[pl.BlockSpec(memory_space=pltpu.SMEM)]
        + [pl.BlockSpec(memory_space=pl.ANY)] * 2,
        out_specs=(
            pl.BlockSpec(memory_space=pl.ANY),
            pl.BlockSpec(memory_space=pltpu.VMEM),
        ),
        scratch_shapes=[
            pltpu.VMEM((N_CTR * rb, features), bf16),
            pltpu.VMEM((blocks, width, features), bf16),
            pltpu.VMEM((PIECES, N_ROW, held, features), bf16),
            pltpu.VMEM((PIECES, N_ROW, held, features), bf16),
            *([piece] * 8),
            pltpu.VMEM((N_CTR, PIECES, CANDS * held, rb), f32),
            pltpu.VMEM((4 * N_CTR, rb), f32),
            pltpu.VMEM((N_CTR, CANDS + 1, held, rb), bf16),
            pltpu.VMEM((CANDS * width, features), bf16),
            pltpu.VMEM((N_ROW // 2 * held, N_CTR * rb), bf16),
            pltpu.VMEM((N_ROW, held, features), f32),
            *([pltpu.VMEM((blocks, held, features), bf16)] * 4),
            pltpu.VMEM((N_CTR, 2 * N_CTR, rb), f32),
            pltpu.VMEM((N_CTR, 8, rb), f32),
            pltpu.VMEM((N_CTR, 8, rb), f32),
            pltpu.VMEM((8, 128), jnp.int32),
            pltpu.VMEM((N_CTR, 8, 128), jnp.int32),
            pltpu.VMEM((N_ROW, 8, 128), jnp.int32),
            pltpu.VMEM((8, 128), jnp.int32),
            pltpu.SMEM((N_CTR, 8, 128), jnp.int32),
            pltpu.SMEM((8, 128), jnp.int32),
            dma((4,)),
            dma((N_CTR,)),
            dma((N_CTR,)),
            dma((1,)),
            dma((1,)),
            dma((18,)),
            dma((18,)),
            *([dma((PIECES,))] * 6),
            *([dma((N_CTR,))] * 4),
            dma((PIECES,)),
        ],
        compiler_params=pltpu.CompilerParams(
            collective_id=0, has_side_effects=True, vmem_limit_bytes=60 * 2**20
        ),
    )(candidates, embeddings, centroids)
    return pl.pallas_call(
        hand_over,
        out_shape=(
            jax.ShapeDtypeStruct(centroids.shape, bf16),
            jax.ShapeDtypeStruct((rb,), f32),
        ),
        in_specs=[pl.BlockSpec(memory_space=pl.ANY)] * 2,
        out_specs=(pl.BlockSpec(memory_space=pl.ANY),) * 2,
        scratch_shapes=[
            pltpu.VMEM(centroids.shape, bf16),
            pltpu.VMEM((rb,), f32),
            dma((blocks + 1,)),
            dma((blocks + 1,)),
        ],
    )(renewed, nearest)


def solution(mesh):
    in_specs = (P(("row", "ctr"), None), P("row", "ctr", None), P(("row", "ctr"), None))
    out_specs = (P("row", "ctr", None), P(("row", "ctr")))
    return jax.shard_map(
        on_device, mesh=mesh, in_specs=in_specs, out_specs=out_specs, check_vma=False
    )
```

```python
import functools
import math

import jax
import jax.numpy as jnp
from jax import lax
from jax.experimental import pallas as pl
from jax.experimental.pallas import tpu as pltpu
from jax.sharding import PartitionSpec as P

score_scale = 1.5
epsilon = 1e-06
MESH = pl.DeviceIdType.MESH

N_Z, N_Y, N_C = 4, 4, 2
N_ROW = N_Z * N_Y * N_C
N_CTR = 4
CANDS = 6
PIECES = 4


def shifted(row, k, sign):
    z, y, c = row // 8, (row // 2) % 4, row % 2
    dz, dy, dc = k // 8, (k // 2) % 4, k % 2
    return (
        lax.rem(z + sign * dz + 4, 4) * 8
        + lax.rem(y + sign * dy + 4, 4) * 2
        + lax.rem(c + sign * dc + 2, 2)
    )


def steps(t):
    return lax.rem(t * 5, N_ROW)


def slot_from(owner, row):
    dz = (row // 8 - owner // 8 + 4) % 4
    dy = ((row // 2) % 4 - (owner // 2) % 4 + 4) % 4
    dc = (row % 2 - owner % 2 + 2) % 2
    return (dz * 8 + dy * 2 + dc) * 13 % N_ROW


def kernel(
    lists, emb_in, cent_in,
    new_out, near_out,
    rows, cent, stage, back, b0, b1, b2, b3, b4, c0, c1, c2, c3,
    ex, part, wts, stat, wb, cum, f0, f1, f2, f3, st, bb, rb, mine, ours, asks, info, ours_at, info_at,
    loc_sem, ms, mr, gs, gr, xs, xr, s1, r1, s2, r2, s3, r3, ss, sr, ns, nr, out_sem,
):
    row, ctr = lax.axis_index("row"), lax.axis_index("ctr")
    fetched = (b0, b1, b2, b3, b4)
    landed = (c0, c1, c2, c3)
    fresh = (f0, f1, f2, f3)
    RB = rows.shape[0] // N_CTR
    D = rows.shape[1]
    H = cent.shape[1] // PIECES
    CB = cent.shape[1]
    PARTS = 6
    WIDE = D // 2
    units = [(i, 0, D) for i in range(PIECES - 1)]
    units += [(PIECES - 1, 0, WIDE), (PIECES - 1, WIDE, D)]
    Q = RB // PARTS

    emb_copy = pltpu.make_async_copy(emb_in, rows.at[pl.ds(0, RB)], loc_sem.at[0])
    cent_copy = pltpu.make_async_copy(cent_in, cent, loc_sem.at[1])
    emb_copy.start()
    cent_copy.start()

    barrier = pltpu.get_barrier_semaphore()

    z, y, c = row // 8, (row // 2) % 4, row % 2
    z_at = [lax.rem(z + d, 4) * 8 for d in range(4)]
    y_at = [lax.rem(y + d, 4) * 2 for d in range(4)]
    c_at = [lax.rem(c + d, 2) for d in range(2)]

    def ahead(k):
        return z_at[k // 8] + y_at[(k // 2) % 4] + c_at[k % 2]

    for k in range(1, N_ROW):
        pl.semaphore_signal(barrier, inc=1, device_id=(ahead(k), ctr), device_id_type=MESH)
    for d in range(1, N_CTR):
        pl.semaphore_signal(
            barrier, inc=1, device_id=(row, lax.rem(ctr + d, N_CTR)), device_id_type=MESH
        )

    lane = lax.broadcasted_iota(jnp.int32, (8, 128), 1)
    line = lax.broadcasted_iota(jnp.int32, (8, 128), 0)
    held = cent.shape[0]
    tile = jnp.where(line == 1, CANDS, jnp.where(line == 0, -1, 0))
    for j in range(CANDS):
        owner, block = lists[0, j] // held, lists[0, j] % held
        tile = jnp.where(jnp.logical_and(line == 0, lane == owner), block, tile)
        tile = jnp.where(jnp.logical_and(line == 1, lane == owner), j, tile)
        tile = jnp.where(jnp.logical_and(line == 2, lane == j), slot_from(owner, row), tile)
    ours[0] = tile
    emb_copy.wait()

    def normalise(t, carry):
        place = pl.ds(pl.multiple_of(t * 64, 64), 64)
        values = rows[place, :].astype(jnp.float32)
        scale = lax.rsqrt(jnp.mean(values * values, axis=-1, keepdims=True) + epsilon)
        rows[place, :] = (values * scale).astype(jnp.bfloat16)
        return carry

    lax.fori_loop(0, RB // 64, normalise, 0)
    pl.semaphore_wait(barrier, N_ROW - 1 + N_CTR - 1)
    list_sends = [
        pltpu.make_async_remote_copy(
            src_ref=ours.at[0],
            dst_ref=ours.at[d],
            send_sem=ms.at[d],
            recv_sem=mr.at[d],
            device_id=(row, lax.rem(ctr + d, N_CTR)),
            device_id_type=MESH,
        )
        for d in range(1, N_CTR)
    ]
    for copy in list_sends:
        copy.start()

    right = (row, lax.rem(ctr + 1, N_CTR))
    left = (row, lax.rem(ctr + 3, N_CTR))

    def row_copy(src, dst, p, device, sem):
        return pltpu.make_async_remote_copy(
            src_ref=rows.at[pl.ds(src * RB + p * Q, Q)],
            dst_ref=rows.at[pl.ds(dst * RB + p * Q, Q)],
            send_sem=xs.at[sem],
            recv_sem=xr.at[sem],
            device_id=device,
            device_id_type=MESH,
        )

    to_right = [row_copy(0, 1, p, right, p) for p in range(PARTS)]
    to_left = [row_copy(0, 3, p, left, PARTS + p) for p in range(PARTS)]
    onward = [row_copy(1, 2, p, right, 2 * PARTS + p) for p in range(PARTS // 2)]
    onward += [row_copy(3, 2, p, left, 2 * PARTS + p) for p in range(PARTS // 2, PARTS)]

    def slot_send(src, dst, k, sign, send, recv):
        return pltpu.make_async_remote_copy(
            src_ref=src,
            dst_ref=dst,
            send_sem=send,
            recv_sem=recv,
            device_id=(shifted(row, steps(k), sign), ctr),
            device_id_type=MESH,
        )

    def all_slots(buf_send, buf_recv, send, recv):
        return pltpu.make_async_remote_copy(
            src_ref=buf_send,
            dst_ref=buf_recv,
            send_sem=send,
            recv_sem=recv,
            device_id=(row, ctr),
            device_id_type=MESH,
        )

    others = pl.ds(1, N_ROW - 1)

    def unit_done(u, source, send, recv):
        i, lo, hi = units[u]
        return all_slots(
            source.at[i, others, :, lo:hi], fetched[u].at[others], send.at[u], recv.at[u]
        )

    def sums_done(i):
        return all_slots(stage.at[i, others], landed[i].at[others], s2.at[i], r2.at[i])

    def unit_out(u, source, pick, send, recv):
        i, lo, hi = units[u]

        def one(k, carry):
            source[i, k, :, lo:hi] = pick(i, k, lo, hi)

            @pl.when(k != 0)
            def _():
                slot_send(
                    source.at[i, k, :, lo:hi], fetched[u].at[k], k, 1, send.at[u], recv.at[u]
                ).start()

            return carry

        lax.fori_loop(0, N_ROW, one, 0)
        fetched[u][0] = source[i, 0, :, lo:hi]

    for p in range(2):
        to_right[p].start()
        to_left[PARTS - 1 - p].start()

    for copy in list_sends:
        copy.wait_recv()
    mine[...] = functools.reduce(jnp.maximum, [ours[d] for d in range(N_CTR)])
    asks[0] = mine[...]

    for t in range(1, N_ROW):
        k = t * 5 % N_ROW
        back_k = (4 - k // 8) % 4 * 8 + (4 - (k // 2) % 4) % 4 * 2 + k % 2
        pltpu.make_async_remote_copy(
            src_ref=mine,
            dst_ref=asks.at[t],
            send_sem=gs.at[0],
            recv_sem=gr.at[0],
            device_id=(ahead(back_k), ctr),
            device_id_type=MESH,
        ).start()
    ours_copy = pltpu.make_async_copy(ours, ours_at, loc_sem.at[2])
    ours_copy.start()
    for p in range(2, PARTS):
        to_right[p].start()
        to_left[PARTS - 1 - p].start()

    asked = pltpu.make_async_remote_copy(
        src_ref=asks.at[pl.ds(1, N_ROW - 1)],
        dst_ref=asks.at[pl.ds(1, N_ROW - 1)],
        send_sem=gs.at[0],
        recv_sem=gr.at[0],
        device_id=(row, ctr),
        device_id_type=MESH,
    )
    asked.wait_recv()
    shape = (N_ROW, 128)
    slot = lax.broadcasted_iota(jnp.int32, shape, 0)
    column = lax.broadcasted_iota(jnp.int32, shape, 1)
    table = asks[:, 0, :]
    want = jnp.max(jnp.where(column == row, table, -1), axis=1, keepdims=True)
    want = jnp.broadcast_to(want, shape)
    want_row = jnp.max(jnp.where(column == slot, want, -1), axis=0, keepdims=True)
    key = jnp.where(want < 0, held, want) * N_ROW + slot
    key_row = jnp.max(jnp.where(column == slot, key, -1), axis=0, keepdims=True)
    less = jnp.logical_and(key_row < key, column < N_ROW)
    rank = jnp.sum(jnp.where(less, 1, 0), axis=1, keepdims=True)
    at = rank == column
    info[0:1, :] = want_row
    info[1:2, :] = jnp.sum(jnp.where(at, slot, 0), axis=0, keepdims=True)
    this = jnp.sum(jnp.where(at, want, 0), axis=0, keepdims=True)
    before = jnp.sum(jnp.where(rank + 1 == column, want, 0), axis=0, keepdims=True)
    after_first = lax.broadcasted_iota(jnp.int32, (1, 128), 1) > 0
    info[2:3, :] = jnp.where(jnp.logical_and(this == before, after_first), 1, 0)
    info[3:4, :] = jnp.max(jnp.where(want == column, rank, -1), axis=0, keepdims=True)
    info[4:8, :] = jnp.zeros((4, 128), jnp.int32)
    info_copy = pltpu.make_async_copy(info, info_at, loc_sem.at[3])
    info_copy.start()
    info_copy.wait()
    ours_copy.wait()

    cent_copy.wait()
    def asked_block(i, k, lo, hi):
        return cent[jnp.maximum(info_at[0, k], 0), i * H : (i + 1) * H, lo:hi]

    for u in range(len(units)):
        unit_out(u, stage, asked_block, s1, r1)

    for p in range(PARTS // 2):
        to_right[p].wait_recv()
        onward[p].start()
        to_left[PARTS - 1 - p].wait_recv()
        onward[PARTS - 1 - p].start()
    for p in range(PARTS // 2):
        to_right[PARTS // 2 + p].wait_recv()
        to_left[p].wait_recv()

    AHEAD = PIECES - 1
    G = CANDS * H

    def scores_of(s, step, spans):
        lo, hi = (0, AHEAD) if step == 0 else (AHEAD, PIECES)
        line = 0 if step == 0 else 2 * N_CTR
        used = range(AHEAD) if step == 0 else [AHEAD + step - 1]
        cols = slice(*units[used[0]][1:])

        def pick(j, carry):
            slot = ours_at[s, 2, j]
            for u in used:
                place = pl.ds(pl.multiple_of(units[u][0] * G + j * H, H), H)
                stat[place, cols] = fetched[u][slot]
            return carry

        lax.fori_loop(0, CANDS, pick, 0)

        for start, width in spans:
            place = pl.ds(start, width)
            score = lax.dot_general(
                stat[lo * G : hi * G, cols], rows[pl.ds(s * RB + start, width), cols],
                (((1,), (1,)), ((), ())), preferred_element_type=jnp.float32,
            )
            if step == 1:
                ex[s, AHEAD, :, place] = score
                continue
            if step == 2:
                score = score + ex[s, AHEAD, :, place]
            score = score_scale * score
            top = jnp.max(score, axis=0, keepdims=True)
            power = jnp.exp(score - top)
            ex[s, lo:hi, :, place] = power.reshape(hi - lo, G, width)
            part[line + s : line + s + 1, place] = top
            part[line + N_CTR + s : line + N_CTR + s + 1, place] = jnp.sum(
                power, axis=0, keepdims=True
            )

    def fetch_done(u):
        done = unit_done(u, stage, s1, r1)
        done.wait_send()
        done.wait_recv()

    third = RB // 3
    whole = [(0, RB)]
    outer, middle = [(0, third), (2 * third, third)], [(third, third)]
    for i in range(AHEAD):
        fetch_done(i)
    for s in (0, 1, 3):
        scores_of(s, 0, whole)
    for p in (0, 1, 4, 5):
        onward[p].wait_recv()
    scores_of(2, 0, outer)
    fetch_done(AHEAD)
    for s in (0, 1, 3):
        scores_of(s, 1, whole)
    scores_of(2, 1, outer)
    for p in (2, 3):
        onward[p].wait_recv()
    scores_of(2, 0, middle)
    scores_of(2, 1, middle)
    fetch_done(AHEAD + 1)
    for s in range(N_CTR):
        scores_of(s, 2, whole)
    for copy in to_right + to_left + onward + list_sends:
        copy.wait_send()
    asked.wait_send()

    top_a, top_b = part[0:N_CTR, :], part[2 * N_CTR : 3 * N_CTR, :]
    top = jnp.maximum(top_a, top_b)
    st[0, 0:N_CTR, :] = top
    st[0, N_CTR : 2 * N_CTR, :] = part[N_CTR : 2 * N_CTR, :] * jnp.exp(top_a - top) + part[
        3 * N_CTR : 4 * N_CTR, :
    ] * jnp.exp(top_b - top)

    stat_sends = [
        pltpu.make_async_remote_copy(
            src_ref=st.at[0],
            dst_ref=st.at[d],
            send_sem=ss.at[d],
            recv_sem=sr.at[d],
            device_id=(row, lax.rem(ctr + d, N_CTR)),
            device_id_type=MESH,
        )
        for d in range(1, N_CTR)
    ]
    for copy in stat_sends:
        copy.start()
    for s in range(N_CTR):
        wts[s, CANDS] = jnp.zeros(wts.shape[2:], wts.dtype)
    for copy in stat_sends:
        copy.wait()
    for s in range(N_CTR):
        tops = [st[d, (s - d) % N_CTR : (s - d) % N_CTR + 1, :] for d in range(N_CTR)]
        totals = [
            st[d, N_CTR + (s - d) % N_CTR : N_CTR + (s - d) % N_CTR + 1, :] for d in range(N_CTR)
        ]
        highest = functools.reduce(jnp.maximum, tops)
        total = functools.reduce(
            jnp.add, [total * jnp.exp(top - highest) for top, total in zip(tops, totals)]
        )
        for line in (0, 2 * N_CTR):
            part[line + N_CTR + s : line + N_CTR + s + 1, :] = (
                jnp.exp(part[line + s : line + s + 1, :] - highest) / total
            )

    for i in range(PIECES):
        line = N_CTR if i < AHEAD else 3 * N_CTR
        for s in range(N_CTR):
            factor = part[line + s : line + s + 1, :]

            def weigh(j, carry):
                place = pl.ds(pl.multiple_of(j * H, H), H)
                wts[s, j] = (ex[s, i, place, :] * factor).astype(jnp.bfloat16)
                return carry

            lax.fori_loop(0, CANDS, weigh, 0)
        batch = N_ROW // 2
        for h in range(N_ROW // batch):

            def lay(t, carry):
                owner = shifted(row, steps(h * batch + t), -1)
                for s in range(N_CTR):
                    j = ours_at[s, 1, owner]
                    wb[pl.ds(pl.multiple_of(t * H, H), H), s * RB : (s + 1) * RB] = wts[s, j]
                return carry

            lax.fori_loop(0, batch, lay, 0)

            def multiply(n, carry):
                place = pl.ds(n * WIDE, WIDE) if i == 0 else pl.ds(pl.multiple_of(n * WIDE, WIDE), WIDE)
                total = jnp.dot(
                    wb[0 : batch * H, :], rows[:, place], preferred_element_type=jnp.float32
                )
                stage[i, h * batch : (h + 1) * batch, :, place] = total.reshape(
                    batch, H, WIDE
                ).astype(jnp.bfloat16)
                return carry

            def deliver(lo, hi):
                def one(t, carry):
                    k = h * batch + t

                    @pl.when(k != 0)
                    def _():
                        slot_send(
                            stage.at[i, k, :, lo:hi], landed[i].at[k, :, lo:hi], k, -1,
                            s2.at[i], r2.at[i],
                        ).start()

                    return carry

                lax.fori_loop(0, batch, one, 0)

            if i == 0:
                for n in range(D // WIDE):
                    multiply(n, 0)
                    deliver(n * WIDE, (n + 1) * WIDE)
            else:
                lax.fori_loop(0, D // WIDE, multiply, 0)
                deliver(0, D)
        landed[i][0] = stage[i, 0]

    out_copies = []
    for i in range(PIECES):
        sums_done(i).wait_recv()

        def add(t, total):
            keep = info_at[2, t].astype(jnp.float32)
            total = landed[i][info_at[1, t]].astype(jnp.float32) + total * keep
            cum[t] = total
            return total

        lax.fori_loop(0, N_ROW, add, jnp.zeros((H, D), jnp.float32))

        def renew(b, carry):
            end = info_at[3, b]
            total = cum[jnp.maximum(end, 0)]
            total = jnp.where(end >= 0, total, jnp.zeros_like(total))
            scale = lax.rsqrt(jnp.mean(total * total, axis=-1, keepdims=True) + epsilon)
            fresh[i][b] = (total * scale * (1.0 / math.sqrt(D))).astype(jnp.bfloat16)
            return carry

        lax.fori_loop(0, cent.shape[0], renew, 0)

        def renewed_block(i, k, lo, hi):
            return fresh[i][jnp.maximum(info_at[0, k], 0), :, lo:hi]

        for u in range(len(units)):
            if units[u][0] == i:
                unit_out(u, back, renewed_block, s3, r3)
        out = pltpu.make_async_copy(
            fresh[i], new_out.at[:, pl.ds(i * H, H)], out_sem.at[i]
        )
        out.start()
        out_copies.append(out)

    for u, (i, lo, hi) in enumerate(units):
        unit_done(u, back, s3, r3).wait_recv()
        for s in range(N_CTR):
            for j in range(CANDS):
                stat[j * H : (j + 1) * H, lo:hi] = fetched[u][ours_at[s, 2, j]]
            similar = lax.dot_general(
                stat[0:G, lo:hi], rows[s * RB : (s + 1) * RB, lo:hi], (((1,), (1,)), ((), ())),
                preferred_element_type=jnp.float32,
            )
            if lo == 0 and hi < D:
                ex[s, 0] = similar
                continue
            if lo > 0:
                similar = similar + ex[s, 0]
            best = jnp.max(similar, axis=0, keepdims=True)
            if i > 0:
                best = jnp.maximum(best, bb[s, 0:1, :])
            bb[s] = jnp.broadcast_to(best, bb.shape[1:])
    best_sends = [
        pltpu.make_async_remote_copy(
            src_ref=bb.at[d],
            dst_ref=rb.at[d],
            send_sem=ns.at[d],
            recv_sem=nr.at[d],
            device_id=(row, lax.rem(ctr - d + N_CTR, N_CTR)),
            device_id_type=MESH,
        )
        for d in range(1, N_CTR)
    ]
    for copy in best_sends:
        copy.start()
    for i in range(PIECES):
        sums_done(i).wait_send()
        out_copies[i].wait()
    for u in range(len(units)):
        unit_done(u, back, s3, r3).wait_send()
    for copy in best_sends:
        copy.wait()
    best = bb[0, 0:1, :]
    for d in range(1, N_CTR):
        best = jnp.maximum(best, rb[d, 0:1, :])
    near_out[...] = best.reshape(near_out.shape)


def hand_over(renewed, nearest, new_out, near_out, hold, near_hold, sems, outs):
    blocks = renewed.shape[0]
    ins = [pltpu.make_async_copy(renewed.at[b], hold.at[b], sems.at[b]) for b in range(blocks)]
    ins.append(pltpu.make_async_copy(nearest, near_hold, sems.at[blocks]))
    away = [pltpu.make_async_copy(hold.at[b], new_out.at[b], outs.at[b]) for b in range(blocks)]
    away.append(pltpu.make_async_copy(near_hold, near_out, outs.at[blocks]))
    for copy in ins:
        copy.start()
    for one, two in zip(ins, away):
        one.wait()
        two.start()
    for copy in away:
        copy.wait()


def on_device(embeddings, centroids, candidates):
    blocks, width, features = centroids.shape
    rb = embeddings.shape[0]
    held = width // PIECES
    bf16, f32 = jnp.bfloat16, jnp.float32
    piece = pltpu.VMEM((N_ROW, held, features), bf16)
    half_piece = pltpu.VMEM((N_ROW, held, features // 2), bf16)
    dma = pltpu.SemaphoreType.DMA
    renewed, nearest = pl.pallas_call(
        kernel,
        out_shape=(
            jax.ShapeDtypeStruct(centroids.shape, bf16),
            jax.ShapeDtypeStruct((rb,), f32),
        ),
        in_specs=[pl.BlockSpec(memory_space=pltpu.SMEM)]
        + [pl.BlockSpec(memory_space=pl.ANY)] * 2,
        out_specs=(
            pl.BlockSpec(memory_space=pl.ANY),
            pl.BlockSpec(memory_space=pltpu.VMEM),
        ),
        scratch_shapes=[
            pltpu.VMEM((N_CTR * rb, features), bf16),
            pltpu.VMEM((blocks, width, features), bf16),
            pltpu.VMEM((PIECES, N_ROW, held, features), bf16),
            pltpu.VMEM((PIECES, N_ROW, held, features), bf16),
            *([piece] * 3),
            *([half_piece] * 2),
            *([piece] * 4),
            pltpu.VMEM((N_CTR, PIECES, CANDS * held, rb), f32),
            pltpu.VMEM((4 * N_CTR, rb), f32),
            pltpu.VMEM((N_CTR, CANDS + 1, held, rb), bf16),
            pltpu.VMEM((CANDS * width, features), bf16),
            pltpu.VMEM((N_ROW // 2 * held, N_CTR * rb), bf16),
            pltpu.VMEM((N_ROW, held, features), f32),
            *([pltpu.VMEM((blocks, held, features), bf16)] * 4),
            pltpu.VMEM((N_CTR, 2 * N_CTR, rb), f32),
            pltpu.VMEM((N_CTR, 8, rb), f32),
            pltpu.VMEM((N_CTR, 8, rb), f32),
            pltpu.VMEM((8, 128), jnp.int32),
            pltpu.VMEM((N_CTR, 8, 128), jnp.int32),
            pltpu.VMEM((N_ROW, 8, 128), jnp.int32),
            pltpu.VMEM((8, 128), jnp.int32),
            pltpu.SMEM((N_CTR, 8, 128), jnp.int32),
            pltpu.SMEM((8, 128), jnp.int32),
            dma((4,)),
            dma((N_CTR,)),
            dma((N_CTR,)),
            dma((1,)),
            dma((1,)),
            dma((18,)),
            dma((18,)),
            *([dma((PIECES + 1,))] * 6),
            *([dma((N_CTR,))] * 4),
            dma((PIECES,)),
        ],
        compiler_params=pltpu.CompilerParams(
            collective_id=0, has_side_effects=True, vmem_limit_bytes=60 * 2**20
        ),
    )(candidates, embeddings, centroids)
    return pl.pallas_call(
        hand_over,
        out_shape=(
            jax.ShapeDtypeStruct(centroids.shape, bf16),
            jax.ShapeDtypeStruct((rb,), f32),
        ),
        in_specs=[pl.BlockSpec(memory_space=pl.ANY)] * 2,
        out_specs=(pl.BlockSpec(memory_space=pl.ANY),) * 2,
        scratch_shapes=[
            pltpu.VMEM(centroids.shape, bf16),
            pltpu.VMEM((rb,), f32),
            dma((blocks + 1,)),
            dma((blocks + 1,)),
        ],
    )(renewed, nearest)


def solution(mesh):
    in_specs = (P(("row", "ctr"), None), P("row", "ctr", None), P(("row", "ctr"), None))
    out_specs = (P("row", "ctr", None), P(("row", "ctr")))
    return jax.shard_map(
        on_device, mesh=mesh, in_specs=in_specs, out_specs=out_specs, check_vma=False
    )
```

```python
import functools
import math

import jax
import jax.numpy as jnp
from jax import lax
from jax.experimental import pallas as pl
from jax.experimental.pallas import tpu as pltpu
from jax.sharding import PartitionSpec as P

score_scale = 1.5
epsilon = 1e-06
MESH = pl.DeviceIdType.MESH

N_Z, N_Y, N_C = 4, 4, 2
N_ROW = N_Z * N_Y * N_C
N_CTR = 4
CANDS = 6
PIECES = 4


def shifted(row, k, sign):
    z, y, c = row // 8, (row // 2) % 4, row % 2
    dz, dy, dc = k // 8, (k // 2) % 4, k % 2
    return (
        lax.rem(z + sign * dz + 4, 4) * 8
        + lax.rem(y + sign * dy + 4, 4) * 2
        + lax.rem(c + sign * dc + 2, 2)
    )


def steps(t):
    return lax.rem(t * 27, N_ROW)


def slot_from(owner, row):
    dz = (row // 8 - owner // 8 + 4) % 4
    dy = ((row // 2) % 4 - (owner // 2) % 4 + 4) % 4
    dc = (row % 2 - owner % 2 + 2) % 2
    return (dz * 8 + dy * 2 + dc) * 19 % N_ROW


def kernel(
    lists, emb_in, cent_in,
    new_out, near_out,
    rows, cent, stage, back, b0, b1, b2, b3, b4, c0, c1, c2, c3,
    ex, part, wts, stat, wb, cum, f0, f1, f2, f3, st, bb, rb, mine, ours, asks, info, ours_at, info_at,
    loc_sem, ms, mr, gs, gr, xs, xr, s1, r1, s2, r2, s3, r3, ss, sr, ns, nr, out_sem,
):
    row, ctr = lax.axis_index("row"), lax.axis_index("ctr")
    fetched = (b0, b1, b2, b3, b4)
    landed = (c0, c1, c2, c3)
    fresh = (f0, f1, f2, f3)
    RB = rows.shape[0] // N_CTR
    D = rows.shape[1]
    H = cent.shape[1] // PIECES
    CB = cent.shape[1]
    PARTS = 6
    WIDE = D // 2
    units = [(i, 0, D) for i in range(PIECES - 1)]
    units += [(PIECES - 1, 0, WIDE), (PIECES - 1, WIDE, D)]
    Q = RB // PARTS

    emb_copy = pltpu.make_async_copy(emb_in, rows.at[pl.ds(0, RB)], loc_sem.at[0])
    cent_copy = pltpu.make_async_copy(cent_in, cent, loc_sem.at[1])
    emb_copy.start()
    cent_copy.start()

    barrier = pltpu.get_barrier_semaphore()

    z, y, c = row // 8, (row // 2) % 4, row % 2
    z_at = [lax.rem(z + d, 4) * 8 for d in range(4)]
    y_at = [lax.rem(y + d, 4) * 2 for d in range(4)]
    c_at = [lax.rem(c + d, 2) for d in range(2)]

    def ahead(k):
        return z_at[k // 8] + y_at[(k // 2) % 4] + c_at[k % 2]

    for k in range(1, N_ROW):
        pl.semaphore_signal(barrier, inc=1, device_id=(ahead(k), ctr), device_id_type=MESH)
    for d in range(1, N_CTR):
        pl.semaphore_signal(
            barrier, inc=1, device_id=(row, lax.rem(ctr + d, N_CTR)), device_id_type=MESH
        )

    lane = lax.broadcasted_iota(jnp.int32, (8, 128), 1)
    line = lax.broadcasted_iota(jnp.int32, (8, 128), 0)
    held = cent.shape[0]
    tile = jnp.where(line == 1, CANDS, jnp.where(line == 0, -1, 0))
    for j in range(CANDS):
        owner, block = lists[0, j] // held, lists[0, j] % held
        tile = jnp.where(jnp.logical_and(line == 0, lane == owner), block, tile)
        tile = jnp.where(jnp.logical_and(line == 1, lane == owner), j, tile)
        tile = jnp.where(jnp.logical_and(line == 2, lane == j), slot_from(owner, row), tile)
    ours[0] = tile
    emb_copy.wait()

    def normalise(t, carry):
        place = pl.ds(pl.multiple_of(t * 64, 64), 64)
        values = rows[place, :].astype(jnp.float32)
        scale = lax.rsqrt(jnp.mean(values * values, axis=-1, keepdims=True) + epsilon)
        rows[place, :] = (values * scale).astype(jnp.bfloat16)
        return carry

    lax.fori_loop(0, RB // 64, normalise, 0)
    pl.semaphore_wait(barrier, N_ROW - 1 + N_CTR - 1)
    list_sends = [
        pltpu.make_async_remote_copy(
            src_ref=ours.at[0],
            dst_ref=ours.at[d],
            send_sem=ms.at[d],
            recv_sem=mr.at[d],
            device_id=(row, lax.rem(ctr + d, N_CTR)),
            device_id_type=MESH,
        )
        for d in range(1, N_CTR)
    ]
    for copy in list_sends:
        copy.start()

    right = (row, lax.rem(ctr + 1, N_CTR))
    left = (row, lax.rem(ctr + 3, N_CTR))

    def row_copy(src, dst, p, device, sem):
        return pltpu.make_async_remote_copy(
            src_ref=rows.at[pl.ds(src * RB + p * Q, Q)],
            dst_ref=rows.at[pl.ds(dst * RB + p * Q, Q)],
            send_sem=xs.at[sem],
            recv_sem=xr.at[sem],
            device_id=device,
            device_id_type=MESH,
        )

    to_right = [row_copy(0, 1, p, right, p) for p in range(PARTS)]
    to_left = [row_copy(0, 3, p, left, PARTS + p) for p in range(PARTS)]
    onward = [row_copy(1, 2, p, right, 2 * PARTS + p) for p in range(PARTS // 2)]
    onward += [row_copy(3, 2, p, left, 2 * PARTS + p) for p in range(PARTS // 2, PARTS)]

    def slot_send(src, dst, k, sign, send, recv):
        return pltpu.make_async_remote_copy(
            src_ref=src,
            dst_ref=dst,
            send_sem=send,
            recv_sem=recv,
            device_id=(shifted(row, steps(k), sign), ctr),
            device_id_type=MESH,
        )

    def all_slots(buf_send, buf_recv, send, recv):
        return pltpu.make_async_remote_copy(
            src_ref=buf_send,
            dst_ref=buf_recv,
            send_sem=send,
            recv_sem=recv,
            device_id=(row, ctr),
            device_id_type=MESH,
        )

    others = pl.ds(1, N_ROW - 1)

    def unit_done(u, source, send, recv):
        i, lo, hi = units[u]
        return all_slots(
            source.at[i, others, :, lo:hi], fetched[u].at[others], send.at[u], recv.at[u]
        )

    def sums_done(i):
        return all_slots(stage.at[i, others], landed[i].at[others], s2.at[i], r2.at[i])

    def unit_out(u, source, pick, send, recv):
        i, lo, hi = units[u]

        def one(k, carry):
            source[i, k, :, lo:hi] = pick(i, k, lo, hi)

            @pl.when(k != 0)
            def _():
                slot_send(
                    source.at[i, k, :, lo:hi], fetched[u].at[k], k, 1, send.at[u], recv.at[u]
                ).start()

            return carry

        lax.fori_loop(0, N_ROW, one, 0)
        fetched[u][0] = source[i, 0, :, lo:hi]

    for p in range(2):
        to_right[p].start()
        to_left[PARTS - 1 - p].start()

    for copy in list_sends:
        copy.wait_recv()
    mine[...] = functools.reduce(jnp.maximum, [ours[d] for d in range(N_CTR)])
    asks[0] = mine[...]

    for t in range(1, N_ROW):
        k = t * 27 % N_ROW
        back_k = (4 - k // 8) % 4 * 8 + (4 - (k // 2) % 4) % 4 * 2 + k % 2
        pltpu.make_async_remote_copy(
            src_ref=mine.at[pl.ds(0, 1)],
            dst_ref=asks.at[t, pl.ds(0, 1)],
            send_sem=gs.at[0],
            recv_sem=gr.at[0],
            device_id=(ahead(back_k), ctr),
            device_id_type=MESH,
        ).start()
    ours_copy = pltpu.make_async_copy(ours, ours_at, loc_sem.at[2])
    ours_copy.start()
    for p in range(2, PARTS):
        to_right[p].start()
        to_left[PARTS - 1 - p].start()

    asked = pltpu.make_async_remote_copy(
        src_ref=asks.at[pl.ds(1, N_ROW - 1), pl.ds(0, 1)],
        dst_ref=asks.at[pl.ds(1, N_ROW - 1), pl.ds(0, 1)],
        send_sem=gs.at[0],
        recv_sem=gr.at[0],
        device_id=(row, ctr),
        device_id_type=MESH,
    )
    asked.wait_recv()
    shape = (N_ROW, 128)
    slot = lax.broadcasted_iota(jnp.int32, shape, 0)
    column = lax.broadcasted_iota(jnp.int32, shape, 1)
    table = asks[:, 0, :]
    want = jnp.max(jnp.where(column == row, table, -1), axis=1, keepdims=True)
    want = jnp.broadcast_to(want, shape)
    want_row = jnp.max(jnp.where(column == slot, want, -1), axis=0, keepdims=True)
    key = jnp.where(want < 0, held, want) * N_ROW + slot
    key_row = jnp.max(jnp.where(column == slot, key, -1), axis=0, keepdims=True)
    less = jnp.logical_and(key_row < key, column < N_ROW)
    rank = jnp.sum(jnp.where(less, 1, 0), axis=1, keepdims=True)
    at = rank == column
    info[0:1, :] = want_row
    info[1:2, :] = jnp.sum(jnp.where(at, slot, 0), axis=0, keepdims=True)
    this = jnp.sum(jnp.where(at, want, 0), axis=0, keepdims=True)
    before = jnp.sum(jnp.where(rank + 1 == column, want, 0), axis=0, keepdims=True)
    after_first = lax.broadcasted_iota(jnp.int32, (1, 128), 1) > 0
    info[2:3, :] = jnp.where(jnp.logical_and(this == before, after_first), 1, 0)
    info[3:4, :] = jnp.max(jnp.where(want == column, rank, -1), axis=0, keepdims=True)
    info[4:8, :] = jnp.zeros((4, 128), jnp.int32)
    info_copy = pltpu.make_async_copy(info, info_at, loc_sem.at[3])
    info_copy.start()
    info_copy.wait()
    ours_copy.wait()

    cent_copy.wait()
    def asked_block(i, k, lo, hi):
        return cent[jnp.maximum(info_at[0, k], 0), i * H : (i + 1) * H, lo:hi]

    for u in range(len(units)):
        unit_out(u, stage, asked_block, s1, r1)

    for p in range(PARTS // 2):
        to_right[p].wait_recv()
        onward[p].start()
        to_left[PARTS - 1 - p].wait_recv()
        onward[PARTS - 1 - p].start()
    for p in range(PARTS // 2):
        to_right[PARTS // 2 + p].wait_recv()
        to_left[p].wait_recv()

    AHEAD = PIECES - 1
    G = CANDS * H

    def scores_of(s, step, spans):
        lo, hi = (0, AHEAD) if step == 0 else (AHEAD, PIECES)
        line = 0 if step == 0 else 2 * N_CTR
        used = range(AHEAD) if step == 0 else [AHEAD + step - 1]
        cols = slice(*units[used[0]][1:])

        def pick(j, carry):
            slot = ours_at[s, 2, j]
            for u in used:
                place = pl.ds(pl.multiple_of(units[u][0] * G + j * H, H), H)
                stat[place, cols] = fetched[u][slot]
            return carry

        lax.fori_loop(0, CANDS, pick, 0)

        for start, width in spans:
            place = pl.ds(start, width)
            score = lax.dot_general(
                stat[lo * G : hi * G, cols], rows[pl.ds(s * RB + start, width), cols],
                (((1,), (1,)), ((), ())), preferred_element_type=jnp.float32,
            )
            if step == 1:
                ex[s, AHEAD, :, place] = score
                continue
            if step == 2:
                score = score + ex[s, AHEAD, :, place]
            score = score_scale * score
            top = jnp.max(score, axis=0, keepdims=True)
            power = jnp.exp(score - top)
            ex[s, lo:hi, :, place] = power.reshape(hi - lo, G, width)
            part[line + s : line + s + 1, place] = top
            part[line + N_CTR + s : line + N_CTR + s + 1, place] = jnp.sum(
                power, axis=0, keepdims=True
            )

    def fetch_done(u):
        done = unit_done(u, stage, s1, r1)
        done.wait_send()
        done.wait_recv()

    third = RB // 3
    whole = [(0, RB)]
    outer, middle = [(0, third), (2 * third, third)], [(third, third)]
    for i in range(AHEAD):
        fetch_done(i)
    for s in (0, 1, 3):
        scores_of(s, 0, whole)
    for p in (0, 1, 4, 5):
        onward[p].wait_recv()
    scores_of(2, 0, outer)
    fetch_done(AHEAD)
    for s in (0, 1, 3):
        scores_of(s, 1, whole)
    scores_of(2, 1, outer)
    for p in (2, 3):
        onward[p].wait_recv()
    scores_of(2, 0, middle)
    scores_of(2, 1, middle)
    fetch_done(AHEAD + 1)
    for s in range(N_CTR):
        scores_of(s, 2, whole)
    for copy in to_right + to_left + onward + list_sends:
        copy.wait_send()
    asked.wait_send()

    top_a, top_b = part[0:N_CTR, :], part[2 * N_CTR : 3 * N_CTR, :]
    top = jnp.maximum(top_a, top_b)
    st[0, 0:N_CTR, :] = top
    st[0, N_CTR : 2 * N_CTR, :] = part[N_CTR : 2 * N_CTR, :] * jnp.exp(top_a - top) + part[
        3 * N_CTR : 4 * N_CTR, :
    ] * jnp.exp(top_b - top)

    stat_sends = [
        pltpu.make_async_remote_copy(
            src_ref=st.at[0],
            dst_ref=st.at[d],
            send_sem=ss.at[d],
            recv_sem=sr.at[d],
            device_id=(row, lax.rem(ctr + d, N_CTR)),
            device_id_type=MESH,
        )
        for d in range(1, N_CTR)
    ]
    for copy in stat_sends:
        copy.start()
    for s in range(N_CTR):
        wts[s, CANDS] = jnp.zeros(wts.shape[2:], wts.dtype)
    for copy in stat_sends:
        copy.wait()
    for s in range(N_CTR):
        tops = [st[d, (s - d) % N_CTR : (s - d) % N_CTR + 1, :] for d in range(N_CTR)]
        totals = [
            st[d, N_CTR + (s - d) % N_CTR : N_CTR + (s - d) % N_CTR + 1, :] for d in range(N_CTR)
        ]
        highest = functools.reduce(jnp.maximum, tops)
        total = functools.reduce(
            jnp.add, [total * jnp.exp(top - highest) for top, total in zip(tops, totals)]
        )
        for line in (0, 2 * N_CTR):
            part[line + N_CTR + s : line + N_CTR + s + 1, :] = (
                jnp.exp(part[line + s : line + s + 1, :] - highest) / total
            )

    for i in range(PIECES):
        line = N_CTR if i < AHEAD else 3 * N_CTR
        for s in range(N_CTR):
            factor = part[line + s : line + s + 1, :]

            def weigh(j, carry):
                place = pl.ds(pl.multiple_of(j * H, H), H)
                wts[s, j] = (ex[s, i, place, :] * factor).astype(jnp.bfloat16)
                return carry

            lax.fori_loop(0, CANDS, weigh, 0)
        batch = N_ROW // 2
        for h in range(N_ROW // batch):

            def lay(t, carry):
                owner = shifted(row, steps(h * batch + t), -1)
                for s in range(N_CTR):
                    j = ours_at[s, 1, owner]
                    wb[pl.ds(pl.multiple_of(t * H, H), H), s * RB : (s + 1) * RB] = wts[s, j]
                return carry

            lax.fori_loop(0, batch, lay, 0)

            def multiply(n, carry):
                place = pl.ds(n * WIDE, WIDE) if i == 0 else pl.ds(pl.multiple_of(n * WIDE, WIDE), WIDE)
                total = jnp.dot(
                    wb[0 : batch * H, :], rows[:, place], preferred_element_type=jnp.float32
                )
                stage[i, h * batch : (h + 1) * batch, :, place] = total.reshape(
                    batch, H, WIDE
                ).astype(jnp.bfloat16)
                return carry

            def deliver(lo, hi):
                def one(t, carry):
                    k = h * batch + t

                    @pl.when(k != 0)
                    def _():
                        slot_send(
                            stage.at[i, k, :, lo:hi], landed[i].at[k, :, lo:hi], k, -1,
                            s2.at[i], r2.at[i],
                        ).start()

                    return carry

                lax.fori_loop(0, batch, one, 0)

            if i == 0:
                for n in range(D // WIDE):
                    multiply(n, 0)
                    deliver(n * WIDE, (n + 1) * WIDE)
            else:
                lax.fori_loop(0, D // WIDE, multiply, 0)
                deliver(0, D)
        landed[i][0] = stage[i, 0]

    out_copies = []
    for i in range(PIECES):
        sums_done(i).wait_recv()

        def add(t, total):
            keep = info_at[2, t].astype(jnp.float32)
            total = landed[i][info_at[1, t]].astype(jnp.float32) + total * keep
            cum[t] = total
            return total

        lax.fori_loop(0, N_ROW, add, jnp.zeros((H, D), jnp.float32))

        def renew(b, carry):
            end = info_at[3, b]
            total = cum[jnp.maximum(end, 0)]
            total = jnp.where(end >= 0, total, jnp.zeros_like(total))
            scale = lax.rsqrt(jnp.mean(total * total, axis=-1, keepdims=True) + epsilon)
            fresh[i][b] = (total * scale * (1.0 / math.sqrt(D))).astype(jnp.bfloat16)
            return carry

        lax.fori_loop(0, cent.shape[0], renew, 0)

        def renewed_block(i, k, lo, hi):
            return fresh[i][jnp.maximum(info_at[0, k], 0), :, lo:hi]

        for u in range(len(units)):
            if units[u][0] == i:
                unit_out(u, back, renewed_block, s3, r3)
        out = pltpu.make_async_copy(
            fresh[i], new_out.at[:, pl.ds(i * H, H)], out_sem.at[i]
        )
        out.start()
        out_copies.append(out)

    for u, (i, lo, hi) in enumerate(units):
        unit_done(u, back, s3, r3).wait_recv()
        for s in range(N_CTR):
            for j in range(CANDS):
                stat[j * H : (j + 1) * H, lo:hi] = fetched[u][ours_at[s, 2, j]]
            similar = lax.dot_general(
                stat[0:G, lo:hi], rows[s * RB : (s + 1) * RB, lo:hi], (((1,), (1,)), ((), ())),
                preferred_element_type=jnp.float32,
            )
            if lo == 0 and hi < D:
                ex[s, 0] = similar
                continue
            if lo > 0:
                similar = similar + ex[s, 0]
            best = jnp.max(similar, axis=0, keepdims=True)
            if i > 0:
                best = jnp.maximum(best, bb[s, 0:1, :])
            bb[s] = jnp.broadcast_to(best, bb.shape[1:])
    best_sends = [
        pltpu.make_async_remote_copy(
            src_ref=bb.at[d],
            dst_ref=rb.at[d],
            send_sem=ns.at[d],
            recv_sem=nr.at[d],
            device_id=(row, lax.rem(ctr - d + N_CTR, N_CTR)),
            device_id_type=MESH,
        )
        for d in range(1, N_CTR)
    ]
    for copy in best_sends:
        copy.start()
    for i in range(PIECES):
        sums_done(i).wait_send()
        out_copies[i].wait()
    for u in range(len(units)):
        unit_done(u, back, s3, r3).wait_send()
    for copy in best_sends:
        copy.wait()
    best = bb[0, 0:1, :]
    for d in range(1, N_CTR):
        best = jnp.maximum(best, rb[d, 0:1, :])
    near_out[...] = best.reshape(near_out.shape)


def hand_over(renewed, nearest, new_out, near_out, hold, near_hold, sems, outs):
    blocks = renewed.shape[0]
    ins = [pltpu.make_async_copy(renewed.at[b], hold.at[b], sems.at[b]) for b in range(blocks)]
    ins.append(pltpu.make_async_copy(nearest, near_hold, sems.at[blocks]))
    away = [pltpu.make_async_copy(hold.at[b], new_out.at[b], outs.at[b]) for b in range(blocks)]
    away.append(pltpu.make_async_copy(near_hold, near_out, outs.at[blocks]))
    for copy in ins:
        copy.start()
    for one, two in zip(ins, away):
        one.wait()
        two.start()
    for copy in away:
        copy.wait()


def on_device(embeddings, centroids, candidates):
    blocks, width, features = centroids.shape
    rb = embeddings.shape[0]
    held = width // PIECES
    bf16, f32 = jnp.bfloat16, jnp.float32
    piece = pltpu.VMEM((N_ROW, held, features), bf16)
    half_piece = pltpu.VMEM((N_ROW, held, features // 2), bf16)
    dma = pltpu.SemaphoreType.DMA
    renewed, nearest = pl.pallas_call(
        kernel,
        out_shape=(
            jax.ShapeDtypeStruct(centroids.shape, bf16),
            jax.ShapeDtypeStruct((rb,), f32),
        ),
        in_specs=[pl.BlockSpec(memory_space=pltpu.SMEM)]
        + [pl.BlockSpec(memory_space=pl.ANY)] * 2,
        out_specs=(
            pl.BlockSpec(memory_space=pl.ANY),
            pl.BlockSpec(memory_space=pltpu.VMEM),
        ),
        scratch_shapes=[
            pltpu.VMEM((N_CTR * rb, features), bf16),
            pltpu.VMEM((blocks, width, features), bf16),
            pltpu.VMEM((PIECES, N_ROW, held, features), bf16),
            pltpu.VMEM((PIECES, N_ROW, held, features), bf16),
            *([piece] * 3),
            *([half_piece] * 2),
            *([piece] * 4),
            pltpu.VMEM((N_CTR, PIECES, CANDS * held, rb), f32),
            pltpu.VMEM((4 * N_CTR, rb), f32),
            pltpu.VMEM((N_CTR, CANDS + 1, held, rb), bf16),
            pltpu.VMEM((CANDS * width, features), bf16),
            pltpu.VMEM((N_ROW // 2 * held, N_CTR * rb), bf16),
            pltpu.VMEM((N_ROW, held, features), f32),
            *([pltpu.VMEM((blocks, held, features), bf16)] * 4),
            pltpu.VMEM((N_CTR, 2 * N_CTR, rb), f32),
            pltpu.VMEM((N_CTR, 8, rb), f32),
            pltpu.VMEM((N_CTR, 8, rb), f32),
            pltpu.VMEM((8, 128), jnp.int32),
            pltpu.VMEM((N_CTR, 8, 128), jnp.int32),
            pltpu.VMEM((N_ROW, 8, 128), jnp.int32),
            pltpu.VMEM((8, 128), jnp.int32),
            pltpu.SMEM((N_CTR, 8, 128), jnp.int32),
            pltpu.SMEM((8, 128), jnp.int32),
            dma((4,)),
            dma((N_CTR,)),
            dma((N_CTR,)),
            dma((1,)),
            dma((1,)),
            dma((18,)),
            dma((18,)),
            *([dma((PIECES + 1,))] * 6),
            *([dma((N_CTR,))] * 4),
            dma((PIECES,)),
        ],
        compiler_params=pltpu.CompilerParams(
            collective_id=0, has_side_effects=True, vmem_limit_bytes=60 * 2**20
        ),
    )(candidates, embeddings, centroids)
    return pl.pallas_call(
        hand_over,
        out_shape=(
            jax.ShapeDtypeStruct(centroids.shape, bf16),
            jax.ShapeDtypeStruct((rb,), f32),
        ),
        in_specs=[pl.BlockSpec(memory_space=pl.ANY)] * 2,
        out_specs=(pl.BlockSpec(memory_space=pl.ANY),) * 2,
        scratch_shapes=[
            pltpu.VMEM(centroids.shape, bf16),
            pltpu.VMEM((rb,), f32),
            dma((blocks + 1,)),
            dma((blocks + 1,)),
        ],
    )(renewed, nearest)


def solution(mesh):
    in_specs = (P(("row", "ctr"), None), P("row", "ctr", None), P(("row", "ctr"), None))
    out_specs = (P("row", "ctr", None), P(("row", "ctr")))
    return jax.shard_map(
        on_device, mesh=mesh, in_specs=in_specs, out_specs=out_specs, check_vma=False
    )
```

```python
import functools
import math

import jax
import jax.numpy as jnp
from jax import lax
from jax.experimental import pallas as pl
from jax.experimental.pallas import tpu as pltpu
from jax.sharding import PartitionSpec as P

score_scale = 1.5
epsilon = 1e-06
MESH = pl.DeviceIdType.MESH

N_Z, N_Y, N_C = 4, 4, 2
N_ROW = N_Z * N_Y * N_C
N_CTR = 4
CANDS = 6
PIECES = 4


def shifted(row, k, sign):
    z, y, c = row // 8, (row // 2) % 4, row % 2
    dz, dy, dc = k // 8, (k // 2) % 4, k % 2
    return (
        lax.rem(z + sign * dz + 4, 4) * 8
        + lax.rem(y + sign * dy + 4, 4) * 2
        + lax.rem(c + sign * dc + 2, 2)
    )


def steps(t):
    return lax.rem(t * 23, N_ROW)


def slot_from(owner, row):
    dz = (row // 8 - owner // 8 + 4) % 4
    dy = ((row // 2) % 4 - (owner // 2) % 4 + 4) % 4
    dc = (row % 2 - owner % 2 + 2) % 2
    return (dz * 8 + dy * 2 + dc) * 7 % N_ROW


def kernel(
    lists, emb_in, cent_in,
    new_out, near_out,
    rows, cent, stage, back, b0, b1, b2, b3, b4, c0, c1, c2, c3,
    ex, part, wts, stat, wb, cum, f0, f1, f2, f3, st, bb, rb, mine, ours, asks, info, ours_at, info_at,
    loc_sem, ms, mr, gs, gr, xs, xr, s1, r1, s2, r2, s3, r3, ss, sr, ns, nr, out_sem,
):
    row, ctr = lax.axis_index("row"), lax.axis_index("ctr")
    fetched = (b0, b1, b2, b3, b4)
    landed = (c0, c1, c2, c3)
    fresh = (f0, f1, f2, f3)
    RB = rows.shape[0] // N_CTR
    D = rows.shape[1]
    H = cent.shape[1] // PIECES
    CB = cent.shape[1]
    PARTS = 6
    WIDE = D // 2
    units = [(i, 0, D) for i in range(PIECES - 1)]
    units += [(PIECES - 1, 0, WIDE), (PIECES - 1, WIDE, D)]
    Q = RB // PARTS

    emb_copy = pltpu.make_async_copy(emb_in, rows.at[pl.ds(0, RB)], loc_sem.at[0])
    cent_copy = pltpu.make_async_copy(cent_in, cent, loc_sem.at[1])
    emb_copy.start()
    cent_copy.start()

    barrier = pltpu.get_barrier_semaphore()

    z, y, c = row // 8, (row // 2) % 4, row % 2
    z_at = [lax.rem(z + d, 4) * 8 for d in range(4)]
    y_at = [lax.rem(y + d, 4) * 2 for d in range(4)]
    c_at = [lax.rem(c + d, 2) for d in range(2)]

    def ahead(k):
        return z_at[k // 8] + y_at[(k // 2) % 4] + c_at[k % 2]

    for k in range(1, N_ROW):
        pl.semaphore_signal(barrier, inc=1, device_id=(ahead(k), ctr), device_id_type=MESH)
    for d in range(1, N_CTR):
        pl.semaphore_signal(
            barrier, inc=1, device_id=(row, lax.rem(ctr + d, N_CTR)), device_id_type=MESH
        )

    lane = lax.broadcasted_iota(jnp.int32, (8, 128), 1)
    line = lax.broadcasted_iota(jnp.int32, (8, 128), 0)
    held = cent.shape[0]
    tile = jnp.where(line == 1, CANDS, jnp.where(line == 0, -1, 0))
    for j in range(CANDS):
        owner, block = lists[0, j] // held, lists[0, j] % held
        tile = jnp.where(jnp.logical_and(line == 0, lane == owner), block, tile)
        tile = jnp.where(jnp.logical_and(line == 1, lane == owner), j, tile)
        tile = jnp.where(jnp.logical_and(line == 2, lane == j), slot_from(owner, row), tile)
    ours[0] = tile
    emb_copy.wait()

    def normalise(t, carry):
        place = pl.ds(pl.multiple_of(t * 64, 64), 64)
        values = rows[place, :].astype(jnp.float32)
        scale = lax.rsqrt(jnp.mean(values * values, axis=-1, keepdims=True) + epsilon)
        rows[place, :] = (values * scale).astype(jnp.bfloat16)
        return carry

    lax.fori_loop(0, RB // 64, normalise, 0)
    pl.semaphore_wait(barrier, N_ROW - 1 + N_CTR - 1)
    list_sends = [
        pltpu.make_async_remote_copy(
            src_ref=ours.at[0],
            dst_ref=ours.at[d],
            send_sem=ms.at[d],
            recv_sem=mr.at[d],
            device_id=(row, lax.rem(ctr + d, N_CTR)),
            device_id_type=MESH,
        )
        for d in range(1, N_CTR)
    ]
    for copy in list_sends:
        copy.start()

    right = (row, lax.rem(ctr + 1, N_CTR))
    left = (row, lax.rem(ctr + 3, N_CTR))

    def row_copy(src, dst, p, device, sem):
        return pltpu.make_async_remote_copy(
            src_ref=rows.at[pl.ds(src * RB + p * Q, Q)],
            dst_ref=rows.at[pl.ds(dst * RB + p * Q, Q)],
            send_sem=xs.at[sem],
            recv_sem=xr.at[sem],
            device_id=device,
            device_id_type=MESH,
        )

    to_right = [row_copy(0, 1, p, right, p) for p in range(PARTS)]
    to_left = [row_copy(0, 3, p, left, PARTS + p) for p in range(PARTS)]
    onward = [row_copy(1, 2, p, right, 2 * PARTS + p) for p in range(PARTS // 2)]
    onward += [row_copy(3, 2, p, left, 2 * PARTS + p) for p in range(PARTS // 2, PARTS)]

    def slot_send(src, dst, k, sign, send, recv):
        return pltpu.make_async_remote_copy(
            src_ref=src,
            dst_ref=dst,
            send_sem=send,
            recv_sem=recv,
            device_id=(shifted(row, steps(k), sign), ctr),
            device_id_type=MESH,
        )

    def all_slots(buf_send, buf_recv, send, recv):
        return pltpu.make_async_remote_copy(
            src_ref=buf_send,
            dst_ref=buf_recv,
            send_sem=send,
            recv_sem=recv,
            device_id=(row, ctr),
            device_id_type=MESH,
        )

    others = pl.ds(1, N_ROW - 1)

    def unit_done(u, source, send, recv):
        i, lo, hi = units[u]
        return all_slots(
            source.at[i, others, :, lo:hi], fetched[u].at[others], send.at[u], recv.at[u]
        )

    def sums_done(i):
        return all_slots(stage.at[i, others], landed[i].at[others], s2.at[i], r2.at[i])

    def unit_out(u, source, pick, send, recv):
        i, lo, hi = units[u]

        def one(k, carry):
            source[i, k, :, lo:hi] = pick(i, k, lo, hi)

            @pl.when(k != 0)
            def _():
                slot_send(
                    source.at[i, k, :, lo:hi], fetched[u].at[k], k, 1, send.at[u], recv.at[u]
                ).start()

            return carry

        lax.fori_loop(0, N_ROW, one, 0)
        fetched[u][0] = source[i, 0, :, lo:hi]

    for p in range(2):
        to_right[p].start()
        to_left[PARTS - 1 - p].start()

    for copy in list_sends:
        copy.wait_recv()
    mine[...] = functools.reduce(jnp.maximum, [ours[d] for d in range(N_CTR)])
    asks[0] = mine[...]

    for t in range(1, N_ROW):
        k = t * 23 % N_ROW
        back_k = (4 - k // 8) % 4 * 8 + (4 - (k // 2) % 4) % 4 * 2 + k % 2
        pltpu.make_async_remote_copy(
            src_ref=mine.at[pl.ds(0, 1)],
            dst_ref=asks.at[t, pl.ds(0, 1)],
            send_sem=gs.at[0],
            recv_sem=gr.at[0],
            device_id=(ahead(back_k), ctr),
            device_id_type=MESH,
        ).start()
    ours_copy = pltpu.make_async_copy(ours, ours_at, loc_sem.at[2])
    ours_copy.start()
    for p in range(2, PARTS):
        to_right[p].start()
        to_left[PARTS - 1 - p].start()

    asked = pltpu.make_async_remote_copy(
        src_ref=asks.at[pl.ds(1, N_ROW - 1), pl.ds(0, 1)],
        dst_ref=asks.at[pl.ds(1, N_ROW - 1), pl.ds(0, 1)],
        send_sem=gs.at[0],
        recv_sem=gr.at[0],
        device_id=(row, ctr),
        device_id_type=MESH,
    )
    asked.wait_recv()
    shape = (N_ROW, 128)
    slot = lax.broadcasted_iota(jnp.int32, shape, 0)
    column = lax.broadcasted_iota(jnp.int32, shape, 1)
    table = asks[:, 0, :]
    want = jnp.max(jnp.where(column == row, table, -1), axis=1, keepdims=True)
    want = jnp.broadcast_to(want, shape)
    want_row = jnp.max(jnp.where(column == slot, want, -1), axis=0, keepdims=True)
    key = jnp.where(want < 0, held, want) * N_ROW + slot
    key_row = jnp.max(jnp.where(column == slot, key, -1), axis=0, keepdims=True)
    less = jnp.logical_and(key_row < key, column < N_ROW)
    rank = jnp.sum(jnp.where(less, 1, 0), axis=1, keepdims=True)
    at = rank == column
    info[0:1, :] = want_row
    info[1:2, :] = jnp.sum(jnp.where(at, slot, 0), axis=0, keepdims=True)
    this = jnp.sum(jnp.where(at, want, 0), axis=0, keepdims=True)
    before = jnp.sum(jnp.where(rank + 1 == column, want, 0), axis=0, keepdims=True)
    after_first = lax.broadcasted_iota(jnp.int32, (1, 128), 1) > 0
    info[2:3, :] = jnp.where(jnp.logical_and(this == before, after_first), 1, 0)
    info[3:4, :] = jnp.max(jnp.where(want == column, rank, -1), axis=0, keepdims=True)
    info[4:8, :] = jnp.zeros((4, 128), jnp.int32)
    info_copy = pltpu.make_async_copy(info, info_at, loc_sem.at[3])
    info_copy.start()
    info_copy.wait()
    ours_copy.wait()

    cent_copy.wait()
    def asked_block(i, k, lo, hi):
        return cent[jnp.maximum(info_at[0, k], 0), i * H : (i + 1) * H, lo:hi]

    for u in range(len(units)):
        unit_out(u, stage, asked_block, s1, r1)

    for p in range(PARTS // 2):
        to_right[p].wait_recv()
        onward[p].start()
        to_left[PARTS - 1 - p].wait_recv()
        onward[PARTS - 1 - p].start()
    for p in range(PARTS // 2):
        to_right[PARTS // 2 + p].wait_recv()
        to_left[p].wait_recv()

    AHEAD = PIECES - 1
    G = CANDS * H

    def scores_of(s, step, spans):
        lo, hi = (0, AHEAD) if step == 0 else (AHEAD, PIECES)
        line = 0 if step == 0 else 2 * N_CTR
        used = range(AHEAD) if step == 0 else [AHEAD + step - 1]
        cols = slice(*units[used[0]][1:])

        def pick(j, carry):
            slot = ours_at[s, 2, j]
            for u in used:
                place = pl.ds(pl.multiple_of(units[u][0] * G + j * H, H), H)
                stat[place, cols] = fetched[u][slot]
            return carry

        lax.fori_loop(0, CANDS, pick, 0)

        for start, width in spans:
            place = pl.ds(start, width)
            score = lax.dot_general(
                stat[lo * G : hi * G, cols], rows[pl.ds(s * RB + start, width), cols],
                (((1,), (1,)), ((), ())), preferred_element_type=jnp.float32,
            )
            if step == 1:
                ex[s, AHEAD, :, place] = score
                continue
            if step == 2:
                score = score + ex[s, AHEAD, :, place]
            score = score_scale * score
            top = jnp.max(score, axis=0, keepdims=True)
            power = jnp.exp(score - top)
            ex[s, lo:hi, :, place] = power.reshape(hi - lo, G, width)
            part[line + s : line + s + 1, place] = top
            part[line + N_CTR + s : line + N_CTR + s + 1, place] = jnp.sum(
                power, axis=0, keepdims=True
            )

    def fetch_done(u):
        done = unit_done(u, stage, s1, r1)
        done.wait_send()
        done.wait_recv()

    third = RB // 3
    whole = [(0, RB)]
    outer, middle = [(0, third), (2 * third, third)], [(third, third)]
    for i in range(AHEAD):
        fetch_done(i)
    for s in (0, 1, 3):
        scores_of(s, 0, whole)
    for p in (0, 1, 4, 5):
        onward[p].wait_recv()
    scores_of(2, 0, outer)
    fetch_done(AHEAD)
    for s in (0, 1, 3):
        scores_of(s, 1, whole)
    scores_of(2, 1, outer)
    for p in (2, 3):
        onward[p].wait_recv()
    scores_of(2, 0, middle)
    scores_of(2, 1, middle)
    fetch_done(AHEAD + 1)
    for s in range(N_CTR):
        scores_of(s, 2, whole)
    for copy in to_right + to_left + onward + list_sends:
        copy.wait_send()
    asked.wait_send()

    top_a, top_b = part[0:N_CTR, :], part[2 * N_CTR : 3 * N_CTR, :]
    top = jnp.maximum(top_a, top_b)
    st[0, 0:N_CTR, :] = top
    st[0, N_CTR : 2 * N_CTR, :] = part[N_CTR : 2 * N_CTR, :] * jnp.exp(top_a - top) + part[
        3 * N_CTR : 4 * N_CTR, :
    ] * jnp.exp(top_b - top)

    stat_sends = [
        pltpu.make_async_remote_copy(
            src_ref=st.at[0],
            dst_ref=st.at[d],
            send_sem=ss.at[d],
            recv_sem=sr.at[d],
            device_id=(row, lax.rem(ctr + d, N_CTR)),
            device_id_type=MESH,
        )
        for d in range(1, N_CTR)
    ]
    for copy in stat_sends:
        copy.start()
    for s in range(N_CTR):
        wts[s, CANDS] = jnp.zeros(wts.shape[2:], wts.dtype)
    for copy in stat_sends:
        copy.wait()
    for s in range(N_CTR):
        tops = [st[d, (s - d) % N_CTR : (s - d) % N_CTR + 1, :] for d in range(N_CTR)]
        totals = [
            st[d, N_CTR + (s - d) % N_CTR : N_CTR + (s - d) % N_CTR + 1, :] for d in range(N_CTR)
        ]
        highest = functools.reduce(jnp.maximum, tops)
        total = functools.reduce(
            jnp.add, [total * jnp.exp(top - highest) for top, total in zip(tops, totals)]
        )
        for line in (0, 2 * N_CTR):
            part[line + N_CTR + s : line + N_CTR + s + 1, :] = (
                jnp.exp(part[line + s : line + s + 1, :] - highest) / total
            )

    for i in range(PIECES):
        line = N_CTR if i < AHEAD else 3 * N_CTR
        for s in range(N_CTR):
            factor = part[line + s : line + s + 1, :]

            def weigh(j, carry):
                place = pl.ds(pl.multiple_of(j * H, H), H)
                wts[s, j] = (ex[s, i, place, :] * factor).astype(jnp.bfloat16)
                return carry

            lax.fori_loop(0, CANDS, weigh, 0)
        batch = N_ROW // 2
        for h in range(N_ROW // batch):

            def lay(t, carry):
                owner = shifted(row, steps(h * batch + t), -1)
                for s in range(N_CTR):
                    j = ours_at[s, 1, owner]
                    wb[pl.ds(pl.multiple_of(t * H, H), H), s * RB : (s + 1) * RB] = wts[s, j]
                return carry

            lax.fori_loop(0, batch, lay, 0)

            def multiply(n, carry):
                place = pl.ds(n * WIDE, WIDE) if i == 0 else pl.ds(pl.multiple_of(n * WIDE, WIDE), WIDE)
                total = jnp.dot(
                    wb[0 : batch * H, :], rows[:, place], preferred_element_type=jnp.float32
                )
                stage[i, h * batch : (h + 1) * batch, :, place] = total.reshape(
                    batch, H, WIDE
                ).astype(jnp.bfloat16)
                return carry

            def deliver(lo, hi):
                def one(t, carry):
                    k = h * batch + t

                    @pl.when(k != 0)
                    def _():
                        slot_send(
                            stage.at[i, k, :, lo:hi], landed[i].at[k, :, lo:hi], k, -1,
                            s2.at[i], r2.at[i],
                        ).start()

                    return carry

                lax.fori_loop(0, batch, one, 0)

            if i == 0:
                for n in range(D // WIDE):
                    multiply(n, 0)
                    deliver(n * WIDE, (n + 1) * WIDE)
            else:
                lax.fori_loop(0, D // WIDE, multiply, 0)
                deliver(0, D)
        landed[i][0] = stage[i, 0]

    out_copies = []
    for i in range(PIECES):
        sums_done(i).wait_recv()

        def add(t, total):
            keep = info_at[2, t].astype(jnp.float32)
            total = landed[i][info_at[1, t]].astype(jnp.float32) + total * keep
            cum[t] = total
            return total

        lax.fori_loop(0, N_ROW, add, jnp.zeros((H, D), jnp.float32))

        def renew(b, carry):
            end = info_at[3, b]
            total = cum[jnp.maximum(end, 0)]
            total = jnp.where(end >= 0, total, jnp.zeros_like(total))
            scale = lax.rsqrt(jnp.mean(total * total, axis=-1, keepdims=True) + epsilon)
            fresh[i][b] = (total * scale * (1.0 / math.sqrt(D))).astype(jnp.bfloat16)
            return carry

        lax.fori_loop(0, cent.shape[0], renew, 0)

        def renewed_block(i, k, lo, hi):
            return fresh[i][jnp.maximum(info_at[0, k], 0), :, lo:hi]

        for u in range(len(units)):
            if units[u][0] == i:
                unit_out(u, back, renewed_block, s3, r3)
        out = pltpu.make_async_copy(
            fresh[i], new_out.at[:, pl.ds(i * H, H)], out_sem.at[i]
        )
        out.start()
        out_copies.append(out)

    for u, (i, lo, hi) in enumerate(units):
        unit_done(u, back, s3, r3).wait_recv()
        for s in range(N_CTR):
            for j in range(CANDS):
                stat[j * H : (j + 1) * H, lo:hi] = fetched[u][ours_at[s, 2, j]]
            similar = lax.dot_general(
                stat[0:G, lo:hi], rows[s * RB : (s + 1) * RB, lo:hi], (((1,), (1,)), ((), ())),
                preferred_element_type=jnp.float32,
            )
            if lo == 0 and hi < D:
                ex[s, 0] = similar
                continue
            if lo > 0:
                similar = similar + ex[s, 0]
            best = jnp.max(similar, axis=0, keepdims=True)
            if i > 0:
                best = jnp.maximum(best, bb[s, 0:1, :])
            bb[s] = jnp.broadcast_to(best, bb.shape[1:])
    best_sends = [
        pltpu.make_async_remote_copy(
            src_ref=bb.at[d],
            dst_ref=rb.at[d],
            send_sem=ns.at[d],
            recv_sem=nr.at[d],
            device_id=(row, lax.rem(ctr - d + N_CTR, N_CTR)),
            device_id_type=MESH,
        )
        for d in range(1, N_CTR)
    ]
    for copy in best_sends:
        copy.start()
    for i in range(PIECES):
        sums_done(i).wait_send()
        out_copies[i].wait()
    for u in range(len(units)):
        unit_done(u, back, s3, r3).wait_send()
    for copy in best_sends:
        copy.wait()
    best = bb[0, 0:1, :]
    for d in range(1, N_CTR):
        best = jnp.maximum(best, rb[d, 0:1, :])
    near_out[...] = best.reshape(near_out.shape)


def hand_over(renewed, nearest, new_out, near_out, hold, near_hold, sems, outs):
    blocks = renewed.shape[0] // 2
    two = [pl.ds(2 * b, 2) for b in range(blocks)]
    ins = [pltpu.make_async_copy(renewed.at[p], hold.at[p], sems.at[b]) for b, p in enumerate(two)]
    ins.append(pltpu.make_async_copy(nearest, near_hold, sems.at[blocks]))
    away = [pltpu.make_async_copy(hold.at[p], new_out.at[p], outs.at[b]) for b, p in enumerate(two)]
    away.append(pltpu.make_async_copy(near_hold, near_out, outs.at[blocks]))
    for copy in ins:
        copy.start()
    for inward, outward in zip(ins, away):
        inward.wait()
        outward.start()
    for copy in away:
        copy.wait()


def on_device(embeddings, centroids, candidates):
    blocks, width, features = centroids.shape
    rb = embeddings.shape[0]
    held = width // PIECES
    bf16, f32 = jnp.bfloat16, jnp.float32
    piece = pltpu.VMEM((N_ROW, held, features), bf16)
    half_piece = pltpu.VMEM((N_ROW, held, features // 2), bf16)
    dma = pltpu.SemaphoreType.DMA
    renewed, nearest = pl.pallas_call(
        kernel,
        out_shape=(
            jax.ShapeDtypeStruct(centroids.shape, bf16),
            jax.ShapeDtypeStruct((rb,), f32),
        ),
        in_specs=[pl.BlockSpec(memory_space=pltpu.SMEM)]
        + [pl.BlockSpec(memory_space=pl.ANY)] * 2,
        out_specs=(
            pl.BlockSpec(memory_space=pl.ANY),
            pl.BlockSpec(memory_space=pltpu.VMEM),
        ),
        scratch_shapes=[
            pltpu.VMEM((N_CTR * rb, features), bf16),
            pltpu.VMEM((blocks, width, features), bf16),
            pltpu.VMEM((PIECES, N_ROW, held, features), bf16),
            pltpu.VMEM((PIECES, N_ROW, held, features), bf16),
            *([piece] * 3),
            *([half_piece] * 2),
            *([piece] * 4),
            pltpu.VMEM((N_CTR, PIECES, CANDS * held, rb), f32),
            pltpu.VMEM((4 * N_CTR, rb), f32),
            pltpu.VMEM((N_CTR, CANDS + 1, held, rb), bf16),
            pltpu.VMEM((CANDS * width, features), bf16),
            pltpu.VMEM((N_ROW // 2 * held, N_CTR * rb), bf16),
            pltpu.VMEM((N_ROW, held, features), f32),
            *([pltpu.VMEM((blocks, held, features), bf16)] * 4),
            pltpu.VMEM((N_CTR, 2 * N_CTR, rb), f32),
            pltpu.VMEM((N_CTR, 8, rb), f32),
            pltpu.VMEM((N_CTR, 8, rb), f32),
            pltpu.VMEM((8, 128), jnp.int32),
            pltpu.VMEM((N_CTR, 8, 128), jnp.int32),
            pltpu.VMEM((N_ROW, 8, 128), jnp.int32),
            pltpu.VMEM((8, 128), jnp.int32),
            pltpu.SMEM((N_CTR, 8, 128), jnp.int32),
            pltpu.SMEM((8, 128), jnp.int32),
            dma((4,)),
            dma((N_CTR,)),
            dma((N_CTR,)),
            dma((1,)),
            dma((1,)),
            dma((18,)),
            dma((18,)),
            *([dma((PIECES + 1,))] * 6),
            *([dma((N_CTR,))] * 4),
            dma((PIECES,)),
        ],
        compiler_params=pltpu.CompilerParams(
            collective_id=0, has_side_effects=True, vmem_limit_bytes=60 * 2**20
        ),
    )(candidates, embeddings, centroids)
    return pl.pallas_call(
        hand_over,
        out_shape=(
            jax.ShapeDtypeStruct(centroids.shape, bf16),
            jax.ShapeDtypeStruct((rb,), f32),
        ),
        in_specs=[pl.BlockSpec(memory_space=pl.ANY)] * 2,
        out_specs=(pl.BlockSpec(memory_space=pl.ANY),) * 2,
        scratch_shapes=[
            pltpu.VMEM(centroids.shape, bf16),
            pltpu.VMEM((rb,), f32),
            dma((blocks + 1,)),
            dma((blocks + 1,)),
        ],
    )(renewed, nearest)


def solution(mesh):
    in_specs = (P(("row", "ctr"), None), P("row", "ctr", None), P(("row", "ctr"), None))
    out_specs = (P("row", "ctr", None), P(("row", "ctr")))
    return jax.shard_map(
        on_device, mesh=mesh, in_specs=in_specs, out_specs=out_specs, check_vma=False
    )
```
